256 devices in a mesh: gx: 16 (over z, core), gy: 16 (over y, x).
Axes of the slice: x: 4, y: 4, z: 8, core: 2. Of those that a mesh axis runs over, the one named last changes fastest.
Arguments:
- density: float32 [1024, 512, 128], P('gx', 'gy'), may hold values from -5 to 5
Outputs:
- potential: float32 [1024, 512, 128], P('gx', 'gy')
- residual: float32 [1024, 512, 128], P('gx', 'gy')
The draws below stay inside these ranges and needn't reach their ends.
All inputs are finite; a program needn't handle non-finite values.
Results may differ from the reference program's by a relative error of at most 0.0004.
Values sent between devices are 32-bit elements; how exact they have to be, the bound alone decides.
A program may use at most 192 MiB of HBM per device.

```python
import math
import jax
import jax.numpy as jnp

NZ = 128
LEVELS = 4
JACOBI = 20
NX = 1024
NY = 512


def draw_density(key, part):
    key = jax.random.fold_in(key, 7)
    return jnp.clip(jax.random.normal(key, (NX, NY, NZ), jnp.float32), -5.0, 5.0)


def setup_inputs(seed: int = 0) -> dict:
    key_list = jax.random.split(jax.random.key(seed), 2)
    density = draw_density(jax.random.fold_in(key_list[1], 71), 0)
    return dict(density=density)


FOUR_PI = 4.0 * math.pi
WEIGHT_FIRST = 1.0 / (1.25 + 0.75 * math.cos(math.pi / 4.0))
WEIGHT_SECOND = 1.0 / (1.25 - 0.75 * math.cos(math.pi / 4.0))
JACOBI_WEIGHT = 0.8


def stencil(padded, inverse):
    beside_all = jnp.pad(padded, ((0, 0), (0, 0), (1, 1)))
    center = beside_all[1:-1, 1:-1, 1:-1]
    total = beside_all[2:, 1:-1, 1:-1] + beside_all[:-2, 1:-1, 1:-1]
    total = total + beside_all[1:-1, 2:, 1:-1] + beside_all[1:-1, :-2, 1:-1]
    total = total + beside_all[1:-1, 1:-1, 2:] + beside_all[1:-1, 1:-1, :-2]
    return (6.0 * center - total) * inverse


def operate(field, inverse):
    return stencil(jnp.pad(field, ((1, 1), (1, 1), (0, 0))), inverse)


def restrict(field):
    sizex, sizey, sizez = field.shape
    return field.reshape(sizex // 2, 2, sizey // 2, 2, sizez // 2, 2).mean(axis=(1, 3, 5))


def prolong(field):
    sizex, sizey, sizez = field.shape
    wide = jnp.broadcast_to(field[:, None, :, None, :, None], (sizex, 2, sizey, 2, sizez, 2))
    return wide.reshape(2 * sizex, 2 * sizey, 2 * sizez)


def relax(field, source, weight, current):
    scale_now = weight * 4.0 ** current / 6.0
    return field + scale_now * (source - operate(field, 0.25 ** current))


def reference(density):
    source = FOUR_PI * density
    sources = []
    smoothed = []
    for current in range(LEVELS):
        field = jnp.zeros_like(source)
        field = relax(field, source, WEIGHT_FIRST, current)
        field = relax(field, source, WEIGHT_SECOND, current)
        remains = source - operate(field, 0.25 ** current)
        sources.append(source)
        smoothed.append(field)
        source = restrict(remains)
    correction = jnp.zeros_like(source)
    for count in range(JACOBI):
        correction = relax(correction, source, JACOBI_WEIGHT, LEVELS)
    for current in reversed(range(LEVELS)):
        field = smoothed[current] + prolong(correction)
        field = relax(field, sources[current], WEIGHT_FIRST, current)
        field = relax(field, sources[current], WEIGHT_SECOND, current)
        correction = field
    residual = sources[0] - operate(correction, 1.0)
    return correction, residual
```

```python
import functools
import math

import jax
import jax.numpy as jnp
from jax import lax
from jax.experimental import pallas as pl
from jax.experimental.pallas import tpu as pltpu
from jax.sharding import PartitionSpec as P

LEVELS = 4
JACOBI = 20
FOUR_PI = 4.0 * math.pi
WEIGHT_FIRST = 1.0 / (1.25 + 0.75 * math.cos(math.pi / 4.0))
WEIGHT_SECOND = 1.0 / (1.25 - 0.75 * math.cos(math.pi / 4.0))
JACOBI_WEIGHT = 0.8

N = 16
LANES = 128
BX = (64, 32, 16, 8, 4)
BY = (32, 16, 8, 4, 2)
OX = (4, 6, 6, 6)
OY = 8
ROWS = (72, 44, 28, 20)
COLS = (48, 32, 24, 24)
START = 4
WIDE = (40, 24, 16, 16)
SPREAD = (0, 1, 2, 2)
HALO = 5
HALO0 = 4
MESH = pl.DeviceIdType.MESH

AROUND = [(dx, dy) for dx in (-1, 0, 1) for dy in (-1, 0, 1) if (dx, dy) != (0, 0)]
AROUND3 = [(dx, dy) for dx in (-1, 0, 1) for dy in (-2, -1, 0, 1, 2) if (dx, dy) != (0, 0)]
PARTNERS = {1: AROUND, 2: AROUND, 3: AROUND3}
EVERYONE = sorted(
    {(dx % N, dy % N) for dx, dy in AROUND3}
    | {(d, 0) for d in range(1, N)}
    | {(0, d) for d in range(1, N)}
)

KINDS = ["own", "ownx", "b", "x", "f", "e"]
SINGLE = [
    "pairs",
    "packer",
    "spreader",
    "cells4",
    "part4",
    "gathery",
    "strip",
    "gatherx",
    "b4",
    "e4",
    "e4wide",
    "out_pot",
    "out_res",
    "load_sem",
    "out_sem",
    "halo_send",
    "halo_recv",
    "part_send",
    "part_recv",
    "gy_send",
    "gy_recv",
    "gx_send",
    "gx_recv",
]


def overlap(step, block, spread):
    low = max(-spread, step * block - HALO)
    high = min(block + spread, step * block + block + HALO)
    return low, high - low, low - step * block


def lanes_of(shape):
    return lax.broadcasted_iota(jnp.int32, shape, len(shape) - 1)


def along_z(cells, level):
    step = 1 << level
    axis = cells.ndim - 1
    lane = lanes_of(cells.shape)
    below = jnp.where(lane >= step, pltpu.roll(cells, step, axis), 0.0)
    above = jnp.where(lane < LANES - step, pltpu.roll(cells, LANES - step, axis), 0.0)
    return below + above


def pair_z(cells, level):
    step = 1 << level
    axis = cells.ndim - 1
    odd = (lanes_of(cells.shape) >> level) & 1
    other = jnp.where(odd == 0, pltpu.roll(cells, LANES - step, axis), pltpu.roll(cells, step, axis))
    return cells + other


def around(ref, row, count, level, start, wide):
    tall = ref[pl.ds(row - 1, count + 2), start : start + wide, :]
    center = tall[1 : count + 1]
    total = tall[:count] + tall[2:]
    total = total + ref[pl.ds(row, count), start - 1 : start - 1 + wide, :]
    total = total + ref[pl.ds(row, count), start + 1 : start + 1 + wide, :]
    return center, total + along_z(center, level)


def chunks(first, count, size, body):
    assert count % size == 0
    if count == size:
        body(first)
        return

    def step(index, carry):
        body(first + index * size)
        return carry

    lax.fori_loop(0, count // size, step, 0)


def kernel(density, potential, residual, *scratch):
    names = [kind + str(level) for kind in KINDS for level in range(LEVELS)] + SINGLE
    refs = dict(zip(names, scratch))
    inbox = dict(zip([(k, d) for k in (1, 2, 3) for d in PARTNERS[k]], scratch[len(names) :]))
    own = [refs[f"own{k}"] for k in range(4)]
    ownx = [refs[f"ownx{k}"] for k in range(4)]
    b = [refs[f"b{k}"] for k in range(4)]
    x = [refs[f"x{k}"] for k in range(4)]
    f = [refs[f"f{k}"] for k in range(4)]
    e = [refs[f"e{k}"] for k in range(4)]
    pairs, packer, spreader = refs["pairs"], refs["packer"], refs["spreader"]

    gx, gy = lax.axis_index("gx"), lax.axis_index("gy")

    def device(step):
        return {"gx": lax.rem(gx + step[0] + N, N), "gy": lax.rem(gy + step[1] + N, N)}

    barrier = pltpu.get_barrier_semaphore()
    for step in EVERYONE:
        pl.semaphore_signal(barrier, inc=1, device_id=device(step), device_id_type=MESH)

    loads = [
        pltpu.make_async_copy(density, own[0].at[4:68, 8:40, :], refs["load_sem"].at[0]),
        pltpu.make_async_copy(density, b[0].at[4:68, 8:40, :], refs["load_sem"].at[1]),
    ]
    for copy in loads:
        copy.start()

    def zero(ref, rows, cols):
        ref[rows[0] : rows[1], cols[0] : cols[1], :] = jnp.zeros(
            (rows[1] - rows[0], cols[1] - cols[0], LANES), jnp.float32
        )

    for ref in (own[0], ownx[0]):
        zero(ref, (0, 4), (0, 48))
        zero(ref, (68, 72), (0, 48))
        zero(ref, (4, 68), (0, 8))
        zero(ref, (4, 68), (40, 48))
    for level in (1, 2, 3):
        zero(own[level], (0, ROWS[level]), (0, COLS[level]))
        zero(ownx[level], (0, ROWS[level]), (0, COLS[level]))
        zero(b[level], (0, ROWS[level]), (0, COLS[level]))
    row = lax.broadcasted_iota(jnp.int32, (768, LANES), 0)
    col = lax.broadcasted_iota(jnp.int32, (768, LANES), 1)
    hit = ((row & 7) == 0) & (((row >> 4) & 7) == (col & 7)) & ((row >> 7) == (col >> 3))
    packer[...] = jnp.where(hit, 0.125, 0.0)
    row = lax.broadcasted_iota(jnp.int32, (LANES, 768), 0)
    col = lax.broadcasted_iota(jnp.int32, (LANES, 768), 1)
    hit = ((row >> 3) == (col >> 7)) & ((row & 7) == ((col >> 4) & 7))
    spreader[...] = jnp.where(hit, 1.0, 0.0)

    def inside_y(level, start, wide):
        place = lax.broadcasted_iota(jnp.int32, (wide, LANES), 0) + (start - OY) + gy * BY[level]
        return jnp.where((place >= 0) & (place < N * BY[level]), 1.0, 0.0)

    left = jnp.where(gx > 0, 1.0, 0.0)
    right = jnp.where(gx < N - 1, 1.0, 0.0)

    def clip_x(ref, level, halo, start, wide):
        first = OX[level]
        last = first + BX[level]
        ref[first - halo : first, start : start + wide, :] *= left
        ref[last : last + halo, start : start + wide, :] *= right

    def presmooth(source, out, level, halo, size):
        inverse = 0.25**level
        scale_first = WEIGHT_FIRST * 4.0**level / 6.0
        scale_second = WEIGHT_SECOND * 4.0**level / 6.0
        linear = scale_first + scale_second
        mixed = scale_first * scale_second * inverse
        start, wide = START, WIDE[level]
        inside = inside_y(level, start, wide)

        def body(row):
            center, total = around(source, row, size, level, start, wide)
            out[pl.ds(row, size), start : start + wide, :] = (
                (linear - 6.0 * mixed) * center + mixed * total
            ) * inside
        chunks(OX[level] - halo, BX[level] + 2 * halo, size, body)
        clip_x(out, level, halo, start, wide)

    def down(source, field, out, level, first, count, size):
        inverse = 0.25**level
        start, wide = START, WIDE[level]
        half = wide // 2

        def body(coarse):
            row = OX[level] + 2 * coarse
            center, total = around(field, row, 2 * size, level, start, wide)
            rest = source[pl.ds(row, 2 * size), start : start + wide, :] - inverse * (6.0 * center - total)
            rest = rest.reshape(size, 2, wide, LANES)
            pairs[:size, :wide, :] = rest[:, 0] + rest[:, 1]
            both = pairs[:size, pl.ds(0, half, stride=2), :] + pairs[:size, pl.ds(1, half, stride=2), :]
            out(coarse, both, size)

        chunks(first, count, size, body)

    def store_level(level):
        start, wide = OY - 2, WIDE[level - 1] // 2
        inside = inside_y(level, start, wide)

        def out(coarse, both, size):
            own[level][pl.ds(OX[level] + coarse, size), start : start + wide, :] = (
                0.125 * pair_z(both, level - 1) * inside
            )
        return out

    loads[0].wait()
    presmooth(own[0], ownx[0], 0, 1, 6)

    pl.semaphore_wait(barrier, len(EVERYONE))

    def halo_copy(index):
        dx, dy = AROUND[index]
        rows = {1: (BX[0] - HALO0, HALO0, 0), 0: (0, BX[0], HALO0), -1: (0, HALO0, BX[0] + HALO0)}[dx]
        cols = {1: (BY[0] - HALO0, HALO0, OY - HALO0), 0: (0, BY[0], OY), -1: (0, HALO0, OY + BY[0])}[dy]
        return pltpu.make_async_remote_copy(
            src_ref=density.at[rows[0] : rows[0] + rows[1], cols[0] : cols[0] + cols[1], :],
            dst_ref=b[0].at[rows[2] : rows[2] + rows[1], cols[2] : cols[2] + cols[1], :],
            send_sem=refs["halo_send"].at[index],
            recv_sem=refs["halo_recv"].at[index],
            device_id=device((dx, dy)),
            device_id_type=MESH,
        )

    halos = [halo_copy(index) for index in range(len(AROUND))]
    for copy in halos:
        copy.start()

    down(own[0], ownx[0], store_level(1), 0, -1, 34, 2)
    clip_x(own[1], 1, SPREAD[1], OY - 2, WIDE[0] // 2)
    presmooth(own[1], ownx[1], 1, 2, 4)
    down(own[1], ownx[1], store_level(2), 1, -2, 20, 2)
    clip_x(own[2], 2, SPREAD[2], OY - 2, WIDE[1] // 2)
    presmooth(own[2], ownx[2], 2, 3, 11)
    down(own[2], ownx[2], store_level(3), 2, -2, 12, 4)
    clip_x(own[3], 3, SPREAD[3], OY - 2, WIDE[2] // 2)
    presmooth(own[3], ownx[3], 3, 3, 14)

    def store_cells(coarse, both, size):
        for index in range(size):
            refs["cells4"][8 * index : 8 * index + 8, :] = both[index]

    down(own[3], ownx[3], store_cells, 3, -2, 8, 8)
    part = jnp.zeros((8, LANES), jnp.float32)
    for place in range(6):
        part = part + jnp.dot(
            refs["cells4"][pl.ds(place, 8, stride=8), :],
            packer[place * LANES : (place + 1) * LANES, :],
            precision=lax.Precision.HIGHEST,
            preferred_element_type=jnp.float32,
        )
    place_x = lax.broadcasted_iota(jnp.int32, (8, LANES), 0) - 2 + gx * BX[4]
    place_y = (lanes_of((8, LANES)) >> 3) - 2 + gy * BY[4]
    inside = (place_x >= 0) & (place_x < N * BX[4]) & (place_y >= 0) & (place_y < N * BY[4])
    part = jnp.where(inside, part, 0.0)
    refs["part4"][...] = part

    def line_copy(axis, step, slot):
        source, slots = (refs["part4"], refs["gathery"]) if axis == "gy" else (refs["strip"], refs["gatherx"])
        return pltpu.make_async_remote_copy(
            src_ref=source,
            dst_ref=slots.at[slot],
            send_sem=refs[axis + "_send"].at[step],
            recv_sem=refs[axis + "_recv"].at[slot],
            device_id=device((step, 0) if axis == "gx" else (0, step)),
            device_id_type=MESH,
        )

    sent = list(halos)
    for step in range(1, N):
        copy = line_copy("gy", step, gy)
        copy.start()
        sent.append(copy)

    parts = {}
    for index, (level, step) in enumerate([(k, d) for k in (3, 2, 1) for d in PARTNERS[k]]):
        low_x, many_x, _ = overlap(step[0], BX[level], SPREAD[level])
        low_y, many_y, _ = overlap(step[1], BY[level], SPREAD[level])
        copy = pltpu.make_async_remote_copy(
            src_ref=own[level].at[
                OX[level] + low_x : OX[level] + low_x + many_x, OY + low_y : OY + low_y + many_y, :
            ],
            dst_ref=inbox[level, step],
            send_sem=refs["part_send"].at[index],
            recv_sem=refs["part_recv"].at[index],
            device_id=device(step),
            device_id_type=MESH,
        )
        copy.start()
        parts[level, step] = copy
        sent.append(copy)

    loads[1].wait()
    for copy in halos:
        copy.wait_recv()
    b[0][0:4, 4:44, :] *= left
    b[0][68:72, 4:44, :] *= right
    for start in (0, 40):
        inside = inside_y(0, start, 8)

        def clip_y(row, start=start, inside=inside):
            b[0][pl.ds(row, 8), start : start + 8, :] *= inside
        chunks(0, 72, 8, clip_y)
    presmooth(b[0], x[0], 0, 3, 5)

    for step in range(1, N):
        slot = lax.rem(gy + N - step, N)
        line_copy("gy", step, slot).wait_recv()
    refs["gathery"][gy] = refs["part4"][...]
    lane = lanes_of((8, LANES))
    near = jnp.zeros((8, LANES), jnp.float32)
    far = jnp.zeros((8, LANES), jnp.float32)
    for slot in range(N):
        moved = pltpu.roll(refs["gathery"][slot], (16 * slot - 16) % LANES, 1)
        if slot < 7:
            near = near + moved
        elif slot > 8:
            far = far + moved
        else:
            low = jnp.where(lane >= 64, moved, 0.0)
            near = near + low
            far = far + (moved - low)
    refs["strip"][0:8, :] = near
    refs["strip"][8:16, :] = far
    for step in range(1, N):
        copy = line_copy("gx", step, gx)
        copy.start()
        sent.append(copy)

    for level in (3, 2, 1):
        spread = SPREAD[level]
        first_x, first_y = OX[level], OY
        rows = slice(first_x - spread, first_x + BX[level] + spread)
        cols = slice(first_y - spread, first_y + BY[level] + spread)
        b[level][rows, cols, :] = own[level][rows, cols, :]
        for step in PARTNERS[level]:
            parts[level, step].wait_recv()
            _, many_x, to_x = overlap(step[0], BX[level], spread)
            _, many_y, to_y = overlap(step[1], BY[level], spread)
            b[level][
                first_x + to_x : first_x + to_x + many_x, first_y + to_y : first_y + to_y + many_y, :
            ] += inbox[level, step][...]
        cover = BY[level] + 2 * HALO
        inside = inside_y(level, OY - HALO, cover)
        b[level][:, OY - HALO : OY - HALO + cover, :] *= inside
        clip_x(b[level], level, HALO, OY - HALO, cover)
        presmooth(b[level], x[level], level, 4, {3: 8, 2: 8, 1: 4}[level])

    for step in range(1, N):
        slot = lax.rem(gx + N - step, N)
        line_copy("gx", step, slot).wait_recv()
    refs["gatherx"][gx] = refs["strip"][...]
    b4, e4 = refs["b4"], refs["e4"]
    b4[...] = jnp.zeros((160, LANES), jnp.float32)
    e4[...] = jnp.zeros((160, LANES), jnp.float32)
    for slot in range(N):
        for tile in range(2):
            at = 80 * tile + 6 + 4 * slot
            b4[at : at + 8, :] += refs["gatherx"][slot, 8 * tile : 8 * tile + 8, :]

    scale = JACOBI_WEIGHT * 4.0**LEVELS / 6.0
    lane = lanes_of((64, LANES))
    for tile in range(2):
        at = 80 * tile + 8
        b4[at : at + 64, :] *= scale
        e4[at : at + 64, :] = b4[at : at + 64, :]

    def sweep(count, carry):
        tiles = [e4[80 * tile + 8 : 80 * tile + 72, :] for tile in range(2)]
        after = [pltpu.roll(tile, 8, 1) for tile in tiles]
        before = [pltpu.roll(tile, LANES - 8, 1) for tile in tiles]
        beside_y = [
            jnp.where(lane >= 8, after[0], 0.0) + jnp.where(lane < LANES - 8, before[0], before[1]),
            jnp.where(lane >= 8, after[1], after[0]) + jnp.where(lane < LANES - 8, before[1], 0.0),
        ]
        new = []
        for tile in range(2):
            at = 80 * tile + 8
            total = e4[at - 1 : at + 63, :] + e4[at + 1 : at + 65, :] + beside_y[tile]
            total = total + jnp.where((lane & 7) != 0, pltpu.roll(tiles[tile], 1, 1), 0.0)
            total = total + jnp.where((lane & 7) != 7, pltpu.roll(tiles[tile], LANES - 1, 1), 0.0)
            new.append(
                (1.0 - JACOBI_WEIGHT) * tiles[tile] + b4[at : at + 64, :] + (JACOBI_WEIGHT / 6.0) * total
            )
        for tile in range(2):
            e4[80 * tile + 8 : 80 * tile + 72, :] = new[tile]
        return carry

    lax.fori_loop(0, JACOBI - 1, sweep, 0)

    lane = lanes_of((8, LANES))
    back = lax.rem(16 - 16 * gy + 2 * LANES, LANES)
    place = lane + 16 * gy - 16
    near = pltpu.roll(e4[pl.ds(6 + 4 * gx, 8), :], back, 1)
    far = pltpu.roll(e4[pl.ds(86 + 4 * gx, 8), :], back, 1)
    mine = jnp.where((place >= 0) & (place < LANES), near, 0.0)
    mine = jnp.where((place >= LANES) & (place < 2 * LANES), far, mine)
    wide4 = jnp.dot(
        mine, spreader[...], precision=lax.Precision.HIGHEST, preferred_element_type=jnp.float32
    )
    for place in range(6):
        refs["e4wide"][pl.ds(place, 8, stride=8), :] = wide4[:, place * LANES : (place + 1) * LANES]

    def correct(level, first, count, size):
        half = 6 if level == 3 else WIDE[level] // 2

        def body(coarse):
            if level == 3:
                fix = refs["e4wide"][...].reshape(8, 8, LANES)[:, :half]
            else:
                fix = e[level + 1][pl.ds(OX[level + 1] + coarse, size), OY - 2 : OY - 2 + half, :]
            fix = jnp.broadcast_to(fix[:, None], (size, 2, half, LANES)).reshape(2 * size, half, LANES)
            row = OX[level] + 2 * coarse
            for parity in range(2):
                place = (pl.ds(row, 2 * size), pl.ds(START + parity, half, stride=2), slice(None))
                x[level][place] = x[level][place] + fix
        chunks(first, count, size, body)

    def relax(field, out, level, weight, halo, size):
        scale_now = weight * 4.0**level / 6.0
        start, wide = START, WIDE[level]
        inside = inside_y(level, start, wide)

        def body(row):
            center, total = around(field, row, size, level, start, wide)
            source = b[level][pl.ds(row, size), start : start + wide, :]
            out[pl.ds(row, size), start : start + wide, :] = (
                (1.0 - weight) * center + scale_now * source + (weight / 6.0) * total
            ) * inside
        chunks(OX[level] - halo, BX[level] + 2 * halo, size, body)
        clip_x(out, level, halo, start, wide)

    correct(3, -2, 8, 8)
    relax(x[3], f[3], 3, WEIGHT_FIRST, 3, 14)
    relax(f[3], e[3], 3, WEIGHT_SECOND, 2, 12)
    correct(2, -2, 12, 6)
    relax(x[2], f[2], 2, WEIGHT_FIRST, 3, 11)
    relax(f[2], e[2], 2, WEIGHT_SECOND, 2, 10)
    correct(1, -2, 20, 4)
    relax(x[1], f[1], 1, WEIGHT_FIRST, 4, 4)
    relax(f[1], e[1], 1, WEIGHT_SECOND, 2, 4)
    correct(0, -2, 36, 4)
    relax(x[0], f[0], 0, WEIGHT_FIRST, 2, 4)
    relax(f[0], e[0], 0, WEIGHT_SECOND, 1, 6)

    def finish(row):
        center, total = around(e[0], row, 4, 0, OY, BY[0])
        source = b[0][pl.ds(row, 4), OY : OY + BY[0], :]
        refs["out_pot"][pl.ds(row - 4, 4)] = FOUR_PI * center
        refs["out_res"][pl.ds(row - 4, 4)] = FOUR_PI * (source - 6.0 * center + total)

    stores = []
    for quarter in range(4):
        chunks(4 + 16 * quarter, 16, 4, finish)
        for index, (source, target) in enumerate(
            ((refs["out_pot"], potential), (refs["out_res"], residual))
        ):
            rows = pl.ds(16 * quarter, 16)
            copy = pltpu.make_async_copy(source.at[rows], target.at[rows], refs["out_sem"].at[index, quarter])
            copy.start()
            stores.append(copy)

    for copy in sent:
        copy.wait_send()
    for copy in stores:
        copy.wait()


def on_device(density):
    def cells(*shape):
        return pltpu.VMEM(shape + (LANES,), jnp.float32)

    level_arrays = [cells(ROWS[k], COLS[k]) for k in range(4)]
    dma = pltpu.SemaphoreType.DMA
    scratch = level_arrays * 6 + [
        cells(8, 40),
        cells(768),
        pltpu.VMEM((LANES, 768), jnp.float32),
        cells(64),
        cells(8),
        cells(N, 8),
        cells(16),
        cells(N, 16),
        cells(160),
        cells(160),
        cells(64),
        cells(64, 32),
        cells(64, 32),
        dma((2,)),
        dma((2, 4)),
        dma((8,)),
        dma((8,)),
        dma((30,)),
        dma((30,)),
        dma((N,)),
        dma((N,)),
        dma((N,)),
        dma((N,)),
    ]
    for level in (1, 2, 3):
        for step in PARTNERS[level]:
            many_x = overlap(step[0], BX[level], SPREAD[level])[1]
            many_y = overlap(step[1], BY[level], SPREAD[level])[1]
            scratch.append(cells(many_x, many_y))
    return pl.pallas_call(
        kernel,
        out_shape=[jax.ShapeDtypeStruct(density.shape, jnp.float32)] * 2,
        in_specs=[pl.BlockSpec(memory_space=pl.ANY)],
        out_specs=[pl.BlockSpec(memory_space=pl.ANY)] * 2,
        scratch_shapes=scratch,
        compiler_params=pltpu.CompilerParams(
            collective_id=0, has_side_effects=True, vmem_limit_bytes=48 * 2**20
        ),
        name="vcycle",
    )(density)


def solution(mesh):
    return jax.shard_map(
        on_device,
        mesh=mesh,
        in_specs=(P("gx", "gy", None),),
        out_specs=(P("gx", "gy", None), P("gx", "gy", None)),
        check_vma=False,
    )
```

```python
import functools
import math

import jax
import jax.numpy as jnp
from jax import lax
from jax.experimental import pallas as pl
from jax.experimental.pallas import tpu as pltpu
from jax.sharding import PartitionSpec as P

LEVELS = 4
JACOBI = 20
FOUR_PI = 4.0 * math.pi
WEIGHT_FIRST = 1.0 / (1.25 + 0.75 * math.cos(math.pi / 4.0))
WEIGHT_SECOND = 1.0 / (1.25 - 0.75 * math.cos(math.pi / 4.0))
JACOBI_WEIGHT = 0.8

N = 16
LANES = 128
BX = (64, 32, 16, 8, 4)
BY = (32, 16, 8, 4, 2)
OX = (4, 6, 6, 6)
OY = 8
ROWS = (72, 44, 28, 20)
COLS = (48, 32, 24, 24)
START = 4
WIDE = (40, 24, 16, 16)
SPREAD = (0, 1, 2, 2)
HALO = 5
HALO0 = 4
MESH = pl.DeviceIdType.MESH

AROUND = [(dx, dy) for dx in (-1, 0, 1) for dy in (-1, 0, 1) if (dx, dy) != (0, 0)]
AROUND3 = [(dx, dy) for dx in (-1, 0, 1) for dy in (-2, -1, 0, 1, 2) if (dx, dy) != (0, 0)]
PARTNERS = {1: AROUND, 2: AROUND, 3: AROUND3}
EVERYONE = sorted(
    {(dx % N, dy % N) for dx, dy in AROUND3}
    | {(d, 0) for d in range(1, N)}
    | {(0, d) for d in range(1, N)}
)

KINDS = ["own", "ownx", "b", "x", "f", "e"]
SINGLE = [
    "pairs",
    "packer",
    "spreader",
    "cells4",
    "part4",
    "gathery",
    "strip",
    "gatherx",
    "b4",
    "e4",
    "e4wide",
    "out_pot",
    "out_res",
    "load_sem",
    "out_sem",
    "halo_send",
    "halo_recv",
    "part_send",
    "part_recv",
    "gy_send",
    "gy_recv",
    "gx_send",
    "gx_recv",
]


def overlap(step, block, spread):
    low = max(-spread, step * block - HALO)
    high = min(block + spread, step * block + block + HALO)
    return low, high - low, low - step * block


def lanes_of(shape):
    return lax.broadcasted_iota(jnp.int32, shape, len(shape) - 1)


def along_z(cells, level):
    step = 1 << level
    axis = cells.ndim - 1
    lane = lanes_of(cells.shape)
    below = jnp.where(lane >= step, pltpu.roll(cells, step, axis), 0.0)
    above = jnp.where(lane < LANES - step, pltpu.roll(cells, LANES - step, axis), 0.0)
    return below + above


def pair_z(cells, level):
    step = 1 << level
    axis = cells.ndim - 1
    odd = (lanes_of(cells.shape) >> level) & 1
    other = jnp.where(odd == 0, pltpu.roll(cells, LANES - step, axis), pltpu.roll(cells, step, axis))
    return cells + other


def around(ref, row, count, level, start, wide):
    tall = ref[pl.ds(row - 1, count + 2), start : start + wide, :]
    center = tall[1 : count + 1]
    total = tall[:count] + tall[2:]
    total = total + ref[pl.ds(row, count), start - 1 : start - 1 + wide, :]
    total = total + ref[pl.ds(row, count), start + 1 : start + 1 + wide, :]
    return center, total + along_z(center, level)


def chunks(first, count, size, body):
    assert count % size == 0
    for index in range(count // size):
        body(first + index * size)


def kernel(density, potential, residual, *scratch):
    names = [kind + str(level) for kind in KINDS for level in range(LEVELS)] + SINGLE
    refs = dict(zip(names, scratch))
    inbox = dict(zip([(k, d) for k in (1, 2, 3) for d in PARTNERS[k]], scratch[len(names) :]))
    own = [refs[f"own{k}"] for k in range(4)]
    ownx = [refs[f"ownx{k}"] for k in range(4)]
    b = [refs[f"b{k}"] for k in range(4)]
    x = [refs[f"x{k}"] for k in range(4)]
    f = [refs[f"f{k}"] for k in range(4)]
    e = [refs[f"e{k}"] for k in range(4)]
    pairs, packer, spreader = refs["pairs"], refs["packer"], refs["spreader"]

    gx, gy = lax.axis_index("gx"), lax.axis_index("gy")

    def device(step):
        return {"gx": lax.rem(gx + step[0] + N, N), "gy": lax.rem(gy + step[1] + N, N)}

    barrier = pltpu.get_barrier_semaphore()
    for step in EVERYONE:
        pl.semaphore_signal(barrier, inc=1, device_id=device(step), device_id_type=MESH)

    loads = [
        pltpu.make_async_copy(density, own[0].at[4:68, 8:40, :], refs["load_sem"].at[0]),
        pltpu.make_async_copy(density, b[0].at[4:68, 8:40, :], refs["load_sem"].at[1]),
    ]
    for copy in loads:
        copy.start()

    def zero(ref, rows, cols):
        ref[rows[0] : rows[1], cols[0] : cols[1], :] = jnp.zeros(
            (rows[1] - rows[0], cols[1] - cols[0], LANES), jnp.float32
        )

    for ref in (own[0], ownx[0]):
        zero(ref, (0, 4), (0, 48))
        zero(ref, (68, 72), (0, 48))
        zero(ref, (4, 68), (0, 8))
        zero(ref, (4, 68), (40, 48))
    for level in (1, 2, 3):
        zero(own[level], (0, ROWS[level]), (0, COLS[level]))
        zero(ownx[level], (0, ROWS[level]), (0, COLS[level]))
        zero(b[level], (0, ROWS[level]), (0, COLS[level]))
    row = lax.broadcasted_iota(jnp.int32, (768, LANES), 0)
    col = lax.broadcasted_iota(jnp.int32, (768, LANES), 1)
    hit = ((row & 7) == 0) & (((row >> 4) & 7) == (col & 7)) & ((row >> 7) == (col >> 3))
    packer[...] = jnp.where(hit, 0.125, 0.0)
    row = lax.broadcasted_iota(jnp.int32, (LANES, 768), 0)
    col = lax.broadcasted_iota(jnp.int32, (LANES, 768), 1)
    hit = ((row >> 3) == (col >> 7)) & ((row & 7) == ((col >> 4) & 7))
    spreader[...] = jnp.where(hit, 1.0, 0.0)

    def inside_y(level, start, wide):
        place = lax.broadcasted_iota(jnp.int32, (wide, LANES), 0) + (start - OY) + gy * BY[level]
        return jnp.where((place >= 0) & (place < N * BY[level]), 1.0, 0.0)

    left = jnp.where(gx > 0, 1.0, 0.0)
    right = jnp.where(gx < N - 1, 1.0, 0.0)

    def clip_x(ref, level, halo, start, wide):
        first = OX[level]
        last = first + BX[level]
        ref[first - halo : first, start : start + wide, :] *= left
        ref[last : last + halo, start : start + wide, :] *= right

    def presmooth(source, out, level, halo, size):
        inverse = 0.25**level
        scale_first = WEIGHT_FIRST * 4.0**level / 6.0
        scale_second = WEIGHT_SECOND * 4.0**level / 6.0
        linear = scale_first + scale_second
        mixed = scale_first * scale_second * inverse
        start, wide = START, WIDE[level]
        inside = inside_y(level, start, wide)

        def body(row):
            center, total = around(source, row, size, level, start, wide)
            out[pl.ds(row, size), start : start + wide, :] = (
                (linear - 6.0 * mixed) * center + mixed * total
            ) * inside
        chunks(OX[level] - halo, BX[level] + 2 * halo, size, body)
        clip_x(out, level, halo, start, wide)

    def down(source, field, out, level, first, count, size):
        inverse = 0.25**level
        start, wide = START, WIDE[level]
        half = wide // 2

        def body(coarse):
            row = OX[level] + 2 * coarse
            center, total = around(field, row, 2 * size, level, start, wide)
            rest = source[pl.ds(row, 2 * size), start : start + wide, :] - inverse * (6.0 * center - total)
            rest = rest.reshape(size, 2, wide, LANES)
            pairs[:size, :wide, :] = rest[:, 0] + rest[:, 1]
            both = pairs[:size, pl.ds(0, half, stride=2), :] + pairs[:size, pl.ds(1, half, stride=2), :]
            out(coarse, both, size)

        chunks(first, count, size, body)

    def store_level(level):
        start, wide = OY - 2, WIDE[level - 1] // 2
        inside = inside_y(level, start, wide)

        def out(coarse, both, size):
            own[level][pl.ds(OX[level] + coarse, size), start : start + wide, :] = (
                0.125 * pair_z(both, level - 1) * inside
            )
        return out

    loads[0].wait()
    presmooth(own[0], ownx[0], 0, 1, 6)

    pl.semaphore_wait(barrier, len(EVERYONE))

    def halo_copy(index):
        dx, dy = AROUND[index]
        rows = {1: (BX[0] - HALO0, HALO0, 0), 0: (0, BX[0], HALO0), -1: (0, HALO0, BX[0] + HALO0)}[dx]
        cols = {1: (BY[0] - HALO0, HALO0, OY - HALO0), 0: (0, BY[0], OY), -1: (0, HALO0, OY + BY[0])}[dy]
        return pltpu.make_async_remote_copy(
            src_ref=density.at[rows[0] : rows[0] + rows[1], cols[0] : cols[0] + cols[1], :],
            dst_ref=b[0].at[rows[2] : rows[2] + rows[1], cols[2] : cols[2] + cols[1], :],
            send_sem=refs["halo_send"].at[index],
            recv_sem=refs["halo_recv"].at[index],
            device_id=device((dx, dy)),
            device_id_type=MESH,
        )

    halos = [halo_copy(index) for index in range(len(AROUND))]
    for copy in halos:
        copy.start()

    down(own[0], ownx[0], store_level(1), 0, -1, 34, 2)
    clip_x(own[1], 1, SPREAD[1], OY - 2, WIDE[0] // 2)
    presmooth(own[1], ownx[1], 1, 2, 4)
    down(own[1], ownx[1], store_level(2), 1, -2, 20, 2)
    clip_x(own[2], 2, SPREAD[2], OY - 2, WIDE[1] // 2)
    presmooth(own[2], ownx[2], 2, 3, 11)
    down(own[2], ownx[2], store_level(3), 2, -2, 12, 4)
    clip_x(own[3], 3, SPREAD[3], OY - 2, WIDE[2] // 2)
    presmooth(own[3], ownx[3], 3, 3, 14)

    def store_cells(coarse, both, size):
        for index in range(size):
            refs["cells4"][8 * index : 8 * index + 8, :] = both[index]

    down(own[3], ownx[3], store_cells, 3, -2, 8, 8)
    part = jnp.zeros((8, LANES), jnp.float32)
    for place in range(6):
        part = part + jnp.dot(
            refs["cells4"][pl.ds(place, 8, stride=8), :],
            packer[place * LANES : (place + 1) * LANES, :],
            precision=lax.Precision.HIGHEST,
            preferred_element_type=jnp.float32,
        )
    place_x = lax.broadcasted_iota(jnp.int32, (8, LANES), 0) - 2 + gx * BX[4]
    place_y = (lanes_of((8, LANES)) >> 3) - 2 + gy * BY[4]
    inside = (place_x >= 0) & (place_x < N * BX[4]) & (place_y >= 0) & (place_y < N * BY[4])
    part = jnp.where(inside, part, 0.0)
    refs["part4"][...] = part

    def line_copy(axis, step, slot):
        source, slots = (refs["part4"], refs["gathery"]) if axis == "gy" else (refs["strip"], refs["gatherx"])
        return pltpu.make_async_remote_copy(
            src_ref=source,
            dst_ref=slots.at[slot],
            send_sem=refs[axis + "_send"].at[step],
            recv_sem=refs[axis + "_recv"].at[slot],
            device_id=device((step, 0) if axis == "gx" else (0, step)),
            device_id_type=MESH,
        )

    sent = list(halos)
    for step in range(1, N):
        copy = line_copy("gy", step, gy)
        copy.start()
        sent.append(copy)

    parts = {}
    for index, (level, step) in enumerate([(k, d) for k in (3, 2, 1) for d in PARTNERS[k]]):
        low_x, many_x, _ = overlap(step[0], BX[level], SPREAD[level])
        low_y, many_y, _ = overlap(step[1], BY[level], SPREAD[level])
        copy = pltpu.make_async_remote_copy(
            src_ref=own[level].at[
                OX[level] + low_x : OX[level] + low_x + many_x, OY + low_y : OY + low_y + many_y, :
            ],
            dst_ref=inbox[level, step],
            send_sem=refs["part_send"].at[index],
            recv_sem=refs["part_recv"].at[index],
            device_id=device(step),
            device_id_type=MESH,
        )
        copy.start()
        parts[level, step] = copy
        sent.append(copy)

    loads[1].wait()
    for copy in halos:
        copy.wait_recv()
    b[0][0:4, 4:44, :] *= left
    b[0][68:72, 4:44, :] *= right
    for start in (0, 40):
        inside = inside_y(0, start, 8)

        def clip_y(row, start=start, inside=inside):
            b[0][pl.ds(row, 8), start : start + 8, :] *= inside
        chunks(0, 72, 8, clip_y)
    presmooth(b[0], x[0], 0, 3, 5)

    for step in range(1, N):
        slot = lax.rem(gy + N - step, N)
        line_copy("gy", step, slot).wait_recv()
    refs["gathery"][gy] = refs["part4"][...]
    lane = lanes_of((8, LANES))
    near = jnp.zeros((8, LANES), jnp.float32)
    far = jnp.zeros((8, LANES), jnp.float32)
    for slot in range(N):
        moved = pltpu.roll(refs["gathery"][slot], (16 * slot - 16) % LANES, 1)
        if slot < 7:
            near = near + moved
        elif slot > 8:
            far = far + moved
        else:
            low = jnp.where(lane >= 64, moved, 0.0)
            near = near + low
            far = far + (moved - low)
    refs["strip"][0:8, :] = near
    refs["strip"][8:16, :] = far
    for step in range(1, N):
        copy = line_copy("gx", step, gx)
        copy.start()
        sent.append(copy)

    for level in (3, 2, 1):
        spread = SPREAD[level]
        first_x, first_y = OX[level], OY
        rows = slice(first_x - spread, first_x + BX[level] + spread)
        cols = slice(first_y - spread, first_y + BY[level] + spread)
        b[level][rows, cols, :] = own[level][rows, cols, :]
        for step in PARTNERS[level]:
            parts[level, step].wait_recv()
            _, many_x, to_x = overlap(step[0], BX[level], spread)
            _, many_y, to_y = overlap(step[1], BY[level], spread)
            b[level][
                first_x + to_x : first_x + to_x + many_x, first_y + to_y : first_y + to_y + many_y, :
            ] += inbox[level, step][...]
        cover = BY[level] + 2 * HALO
        inside = inside_y(level, OY - HALO, cover)
        b[level][:, OY - HALO : OY - HALO + cover, :] *= inside
        clip_x(b[level], level, HALO, OY - HALO, cover)
        presmooth(b[level], x[level], level, 4, {3: 8, 2: 8, 1: 4}[level])

    for step in range(1, N):
        slot = lax.rem(gx + N - step, N)
        line_copy("gx", step, slot).wait_recv()
    refs["gatherx"][gx] = refs["strip"][...]
    b4, e4 = refs["b4"], refs["e4"]
    b4[...] = jnp.zeros((160, LANES), jnp.float32)
    e4[...] = jnp.zeros((160, LANES), jnp.float32)
    for slot in range(N):
        for tile in range(2):
            at = 80 * tile + 6 + 4 * slot
            b4[at : at + 8, :] += refs["gatherx"][slot, 8 * tile : 8 * tile + 8, :]

    scale = JACOBI_WEIGHT * 4.0**LEVELS / 6.0
    lane = lanes_of((64, LANES))
    for tile in range(2):
        at = 80 * tile + 8
        b4[at : at + 64, :] *= scale
        e4[at : at + 64, :] = b4[at : at + 64, :]

    def sweep(count, carry):
        tiles = [e4[80 * tile + 8 : 80 * tile + 72, :] for tile in range(2)]
        after = [pltpu.roll(tile, 8, 1) for tile in tiles]
        before = [pltpu.roll(tile, LANES - 8, 1) for tile in tiles]
        beside_y = [
            jnp.where(lane >= 8, after[0], 0.0) + jnp.where(lane < LANES - 8, before[0], before[1]),
            jnp.where(lane >= 8, after[1], after[0]) + jnp.where(lane < LANES - 8, before[1], 0.0),
        ]
        new = []
        for tile in range(2):
            at = 80 * tile + 8
            total = e4[at - 1 : at + 63, :] + e4[at + 1 : at + 65, :] + beside_y[tile]
            total = total + jnp.where((lane & 7) != 0, pltpu.roll(tiles[tile], 1, 1), 0.0)
            total = total + jnp.where((lane & 7) != 7, pltpu.roll(tiles[tile], LANES - 1, 1), 0.0)
            new.append(
                (1.0 - JACOBI_WEIGHT) * tiles[tile] + b4[at : at + 64, :] + (JACOBI_WEIGHT / 6.0) * total
            )
        for tile in range(2):
            e4[80 * tile + 8 : 80 * tile + 72, :] = new[tile]
        return carry

    lax.fori_loop(0, JACOBI - 1, sweep, 0)

    lane = lanes_of((8, LANES))
    back = lax.rem(16 - 16 * gy + 2 * LANES, LANES)
    place = lane + 16 * gy - 16
    near = pltpu.roll(e4[pl.ds(6 + 4 * gx, 8), :], back, 1)
    far = pltpu.roll(e4[pl.ds(86 + 4 * gx, 8), :], back, 1)
    mine = jnp.where((place >= 0) & (place < LANES), near, 0.0)
    mine = jnp.where((place >= LANES) & (place < 2 * LANES), far, mine)
    wide4 = jnp.dot(
        mine, spreader[...], precision=lax.Precision.HIGHEST, preferred_element_type=jnp.float32
    )
    for place in range(6):
        refs["e4wide"][pl.ds(place, 8, stride=8), :] = wide4[:, place * LANES : (place + 1) * LANES]

    def correct(level, first, count, size):
        half = 6 if level == 3 else WIDE[level] // 2

        def body(coarse):
            if level == 3:
                fix = refs["e4wide"][...].reshape(8, 8, LANES)[:, :half]
            else:
                fix = e[level + 1][pl.ds(OX[level + 1] + coarse, size), OY - 2 : OY - 2 + half, :]
            fix = jnp.broadcast_to(fix[:, None], (size, 2, half, LANES)).reshape(2 * size, half, LANES)
            row = OX[level] + 2 * coarse
            for parity in range(2):
                place = (pl.ds(row, 2 * size), pl.ds(START + parity, half, stride=2), slice(None))
                x[level][place] = x[level][place] + fix
        chunks(first, count, size, body)

    def relax(field, out, level, weight, halo, size):
        scale_now = weight * 4.0**level / 6.0
        start, wide = START, WIDE[level]
        inside = inside_y(level, start, wide)

        def body(row):
            center, total = around(field, row, size, level, start, wide)
            source = b[level][pl.ds(row, size), start : start + wide, :]
            out[pl.ds(row, size), start : start + wide, :] = (
                (1.0 - weight) * center + scale_now * source + (weight / 6.0) * total
            ) * inside
        chunks(OX[level] - halo, BX[level] + 2 * halo, size, body)
        clip_x(out, level, halo, start, wide)

    correct(3, -2, 8, 8)
    relax(x[3], f[3], 3, WEIGHT_FIRST, 3, 14)
    relax(f[3], e[3], 3, WEIGHT_SECOND, 2, 12)
    correct(2, -2, 12, 6)
    relax(x[2], f[2], 2, WEIGHT_FIRST, 3, 11)
    relax(f[2], e[2], 2, WEIGHT_SECOND, 2, 10)
    correct(1, -2, 20, 4)
    relax(x[1], f[1], 1, WEIGHT_FIRST, 4, 4)
    relax(f[1], e[1], 1, WEIGHT_SECOND, 2, 4)
    correct(0, -2, 36, 4)
    relax(x[0], f[0], 0, WEIGHT_FIRST, 2, 4)
    relax(f[0], e[0], 0, WEIGHT_SECOND, 1, 6)

    def finish(row):
        center, total = around(e[0], row, 4, 0, OY, BY[0])
        source = b[0][pl.ds(row, 4), OY : OY + BY[0], :]
        refs["out_pot"][pl.ds(row - 4, 4)] = FOUR_PI * center
        refs["out_res"][pl.ds(row - 4, 4)] = FOUR_PI * (source - 6.0 * center + total)

    stores = []
    for quarter in range(4):
        chunks(4 + 16 * quarter, 16, 4, finish)
        for index, (source, target) in enumerate(
            ((refs["out_pot"], potential), (refs["out_res"], residual))
        ):
            rows = pl.ds(16 * quarter, 16)
            copy = pltpu.make_async_copy(source.at[rows], target.at[rows], refs["out_sem"].at[index, quarter])
            copy.start()
            stores.append(copy)

    for copy in sent:
        copy.wait_send()
    for copy in stores:
        copy.wait()


def on_device(density):
    def cells(*shape):
        return pltpu.VMEM(shape + (LANES,), jnp.float32)

    level_arrays = [cells(ROWS[k], COLS[k]) for k in range(4)]
    dma = pltpu.SemaphoreType.DMA
    scratch = level_arrays * 6 + [
        cells(8, 40),
        cells(768),
        pltpu.VMEM((LANES, 768), jnp.float32),
        cells(64),
        cells(8),
        cells(N, 8),
        cells(16),
        cells(N, 16),
        cells(160),
        cells(160),
        cells(64),
        cells(64, 32),
        cells(64, 32),
        dma((2,)),
        dma((2, 4)),
        dma((8,)),
        dma((8,)),
        dma((30,)),
        dma((30,)),
        dma((N,)),
        dma((N,)),
        dma((N,)),
        dma((N,)),
    ]
    for level in (1, 2, 3):
        for step in PARTNERS[level]:
            many_x = overlap(step[0], BX[level], SPREAD[level])[1]
            many_y = overlap(step[1], BY[level], SPREAD[level])[1]
            scratch.append(cells(many_x, many_y))
    return pl.pallas_call(
        kernel,
        out_shape=[jax.ShapeDtypeStruct(density.shape, jnp.float32)] * 2,
        in_specs=[pl.BlockSpec(memory_space=pl.ANY)],
        out_specs=[pl.BlockSpec(memory_space=pl.ANY)] * 2,
        scratch_shapes=scratch,
        compiler_params=pltpu.CompilerParams(
            collective_id=0, has_side_effects=True, vmem_limit_bytes=48 * 2**20
        ),
        name="vcycle",
    )(density)


def solution(mesh):
    return jax.shard_map(
        on_device,
        mesh=mesh,
        in_specs=(P("gx", "gy", None),),
        out_specs=(P("gx", "gy", None), P("gx", "gy", None)),
        check_vma=False,
    )
```

```python
import math

import jax
import jax.numpy as jnp
from jax import lax
from jax.experimental import pallas as pl
from jax.experimental.pallas import tpu as pltpu
from jax.sharding import PartitionSpec as P

LEVELS = 4
JACOBI = 20
FOUR_PI = 4.0 * math.pi
WEIGHT_FIRST = 1.0 / (1.25 + 0.75 * math.cos(math.pi / 4.0))
WEIGHT_SECOND = 1.0 / (1.25 - 0.75 * math.cos(math.pi / 4.0))
JACOBI_WEIGHT = 0.8

N = 16
LANES = 128
BX = (64, 32, 16, 8, 4)
BY = (32, 16, 8, 4, 2)
OX = (4, 6, 6, 6)
OY = 8
ROWS = (72, 44, 28, 20)
COLS = (48, 32, 24, 24)
START = 4
WIDE = (40, 24, 16, 16)
SPREAD = (0, 1, 2, 2)
HALO = 5
HALO0 = 4
MESH = pl.DeviceIdType.MESH

AROUND = [(dx, dy) for dx in (-1, 0, 1) for dy in (-1, 0, 1) if (dx, dy) != (0, 0)]
AROUND3 = [(dx, dy) for dx in (-1, 0, 1) for dy in (-2, -1, 0, 1, 2) if (dx, dy) != (0, 0)]
PARTNERS = {1: AROUND, 2: AROUND, 3: AROUND3}
EVERYONE = sorted(
    {(dx % N, dy % N) for dx, dy in AROUND3}
    | {(d, 0) for d in range(1, N)}
    | {(0, d) for d in range(1, N)}
)

KINDS = ["own", "ownx", "b", "x", "f", "e"]
SINGLE = [
    "pairs",
    "packer",
    "spreader",
    "cells4",
    "part4",
    "gathery",
    "strip",
    "gatherx",
    "b4",
    "e4wide",
    "sines_x",
    "sines_yz",
    "gains",
    "load_sem",
    "halo_send",
    "halo_recv",
    "part_send",
    "part_recv",
    "gy_send",
    "gy_recv",
    "gx_send",
    "gx_recv",
]


def sine_table(row, col, count):
    period = 2.0 * (count + 1)
    turns = (row + 1.0) * (col + 1.0)
    turns = turns - period * jnp.floor((turns + 0.5) * (1.0 / period))
    turns = turns - (count + 1.0)
    size = jnp.abs(turns)
    size = jnp.minimum(size, (count + 1.0) - size)
    angle = size * (math.pi / (count + 1))
    square = angle * angle
    total = 1.0
    for order in (12, 10, 8, 6, 4, 2):
        total = 1.0 - total * square * (1.0 / (order * (order + 1)))
    value = angle * total * math.sqrt(2.0 / (count + 1))
    return jnp.where(turns < 0.0, value, -value)


def coarse_tables(sines_x, sines_yz, gains):
    def places(shape):
        return [lax.broadcasted_iota(jnp.int32, shape, axis) for axis in range(2)]

    def real(numbers):
        return numbers.astype(jnp.float32)

    row, col = places((80, LANES))
    inside = (row >= 8) & (row < 72) & (col < 64)
    sines_x[...] = jnp.where(inside, sine_table(real(row - 8), real(col), 64), 0.0)
    for tile in range(8):
        row, col = places((32, 256))
        row = row + 32 * tile
        sines_yz[32 * tile : 32 * tile + 32, :] = sine_table(
            real(row >> 3), real(col >> 3), 32
        ) * sine_table(real(row & 7), real(col & 7), 8)

    def value(place, count):
        sine = sine_table(real(place), jnp.zeros(place.shape, jnp.float32), 2 * count + 1)
        return (4.0 * (count + 1)) * sine * sine

    row, col = places((64, 256))
    damped = (JACOBI_WEIGHT / 6.0) * (value(row, 64) + value(col >> 3, 32) + value(col & 7, 8))
    kept = 1.0 - damped
    power = kept * kept
    power = power * power
    fourth = power
    power = power * power
    power = power * power * fourth
    assert JACOBI == 20
    gains[...] = (JACOBI_WEIGHT * 4.0**LEVELS / 6.0) * (1.0 - power) / damped


def ring(step, count):
    return min(step % count, -step % count)


def hops_x(step):
    return sum(ring((core + step) // 2 - core // 2, 8) for core in range(2))


def hops_y(step):
    return sum(ring((x + step) // 4, 4) + ring((x + step) % 4 - x, 4) for x in range(4))


FAR_FIRST = {
    "gx": sorted(range(1, N), key=hops_x, reverse=True),
    "gy": sorted(range(1, N), key=hops_y, reverse=True),
}


def overlap(step, block, spread):
    low = max(-spread, step * block - HALO)
    high = min(block + spread, step * block + block + HALO)
    return low, high - low, low - step * block


def lanes_of(shape):
    return lax.broadcasted_iota(jnp.int32, shape, len(shape) - 1)


def along_z(cells, level):
    step = 1 << level
    axis = cells.ndim - 1
    lane = lanes_of(cells.shape)
    below = jnp.where(lane >= step, pltpu.roll(cells, step, axis), 0.0)
    above = jnp.where(lane < LANES - step, pltpu.roll(cells, LANES - step, axis), 0.0)
    return below + above


def pair_z(cells, level):
    step = 1 << level
    axis = cells.ndim - 1
    odd = (lanes_of(cells.shape) >> level) & 1
    other = jnp.where(odd == 0, pltpu.roll(cells, LANES - step, axis), pltpu.roll(cells, step, axis))
    return cells + other


def around(ref, row, count, level, start, wide):
    tall = ref[pl.ds(row - 1, count + 2), start : start + wide, :]
    center = tall[1 : count + 1]
    total = tall[:count] + tall[2:]
    total = total + ref[pl.ds(row, count), start - 1 : start - 1 + wide, :]
    total = total + ref[pl.ds(row, count), start + 1 : start + 1 + wide, :]
    return center, total + along_z(center, level)


def inside_y(level, start, wide, scale=1.0):
    place = lax.broadcasted_iota(jnp.int32, (wide, LANES), 0) + (start - OY)
    place = place + lax.axis_index("gy") * BY[level]
    return jnp.where((place >= 0) & (place < N * BY[level]), scale, 0.0)


def clip_x(ref, level, halo, start, wide):
    gx = lax.axis_index("gx")
    first = OX[level]
    last = first + BX[level]
    ref[first - halo : first, start : start + wide, :] *= jnp.where(gx > 0, 1.0, 0.0)
    ref[last : last + halo, start : start + wide, :] *= jnp.where(gx < N - 1, 1.0, 0.0)


def chunks(first, count, size, body):
    assert count % size == 0
    for index in range(count // size):
        body(first + index * size)


def kernel(density, e1_out, relaxed_low, relaxed_high, source_low, source_high, *scratch):
    names = [kind + str(level) for kind in KINDS for level in range(LEVELS)] + SINGLE
    refs = dict(zip(names, scratch))
    inbox = dict(zip([(k, d) for k in (1, 2, 3) for d in PARTNERS[k]], scratch[len(names) :]))
    own = [refs[f"own{k}"] for k in range(4)]
    ownx = [refs[f"ownx{k}"] for k in range(4)]
    b = [refs[f"b{k}"] for k in range(4)]
    x = [refs[f"x{k}"] for k in range(4)]
    f = [refs[f"f{k}"] for k in range(4)]
    e = [None, e1_out, refs["e2"], refs["e3"]]
    pairs, packer, spreader = refs["pairs"], refs["packer"], refs["spreader"]

    gx, gy = lax.axis_index("gx"), lax.axis_index("gy")

    def device(step):
        return {"gx": lax.rem(gx + step[0] + N, N), "gy": lax.rem(gy + step[1] + N, N)}

    barrier = pltpu.get_barrier_semaphore()
    for step in EVERYONE:
        pl.semaphore_signal(barrier, inc=1, device_id=device(step), device_id_type=MESH)

    loads = [
        pltpu.make_async_copy(
            density.at[16 * part : 16 * part + 16],
            own[0].at[4 + 16 * part : 20 + 16 * part, 8:40, :],
            refs["load_sem"].at[part],
        )
        for part in range(4)
    ]
    later = pltpu.make_async_copy(density, b[0].at[4:68, 8:40, :], refs["load_sem"].at[4])
    for copy in loads + [later]:
        copy.start()

    def zero(ref, rows, cols):
        ref[rows[0] : rows[1], cols[0] : cols[1], :] = jnp.zeros(
            (rows[1] - rows[0], cols[1] - cols[0], LANES), jnp.float32
        )

    for ref in (own[0], ownx[0]):
        zero(ref, (0, 4), (0, 48))
        zero(ref, (68, 72), (0, 48))
        zero(ref, (4, 68), (0, 8))
        zero(ref, (4, 68), (40, 48))
    for level in (1, 2, 3):
        zero(own[level], (0, ROWS[level]), (0, COLS[level]))
        zero(ownx[level], (0, ROWS[level]), (0, COLS[level]))
        zero(b[level], (0, ROWS[level]), (0, COLS[level]))
    row = lax.broadcasted_iota(jnp.int32, (768, LANES), 0)
    col = lax.broadcasted_iota(jnp.int32, (768, LANES), 1)
    hit = ((row & 7) == 0) & (((row >> 4) & 7) == (col & 7)) & ((row >> 7) == (col >> 3))
    packer[...] = jnp.where(hit, 0.125, 0.0)
    row = lax.broadcasted_iota(jnp.int32, (LANES, 768), 0)
    col = lax.broadcasted_iota(jnp.int32, (LANES, 768), 1)
    hit = ((row >> 3) == (col >> 7)) & ((row & 7) == ((col >> 4) & 7))
    spreader[...] = jnp.where(hit, 1.0, 0.0)

    def presmooth(source, out, level, halo, size, ready=None):
        inverse = 0.25**level
        scale_first = WEIGHT_FIRST * 4.0**level / 6.0
        scale_second = WEIGHT_SECOND * 4.0**level / 6.0
        linear = scale_first + scale_second
        mixed = scale_first * scale_second * inverse
        start, wide = START, WIDE[level]
        inside = inside_y(level, start, wide)

        def body(row):
            if ready is not None:
                ready(row + size)
            center, total = around(source, row, size, level, start, wide)
            out[pl.ds(row, size), start : start + wide, :] = (
                (linear - 6.0 * mixed) * center + mixed * total
            ) * inside
        chunks(OX[level] - halo, BX[level] + 2 * halo, size, body)
        clip_x(out, level, halo, start, wide)

    def down(source, field, out, level, first, count, size):
        inverse = 0.25**level
        start, wide = START, WIDE[level]
        half = wide // 2

        def body(coarse):
            row = OX[level] + 2 * coarse
            center, total = around(field, row, 2 * size, level, start, wide)
            rest = source[pl.ds(row, 2 * size), start : start + wide, :] - inverse * (6.0 * center - total)
            rest = rest.reshape(size, 2, wide, LANES)
            at = pl.ds(coarse - first, size)
            pairs[at, :wide, :] = rest[:, 0] + rest[:, 1]
            both = pairs[at, pl.ds(0, half, stride=2), :] + pairs[at, pl.ds(1, half, stride=2), :]
            out(coarse, both, size)

        chunks(first, count, size, body)

    def store_level(level):
        start, wide = OY - 2, WIDE[level - 1] // 2
        inside = inside_y(level, start, wide)

        def out(coarse, both, size):
            own[level][pl.ds(OX[level] + coarse, size), start : start + wide, :] = (
                0.125 * pair_z(both, level - 1) * inside
            )
        return out

    waiting = list(loads)

    def loaded(row):
        while waiting and (row >= 4 + 16 * (4 - len(waiting)) or row >= 67):
            waiting.pop(0).wait()

    presmooth(own[0], ownx[0], 0, 1, 11, loaded)

    pl.semaphore_wait(barrier, len(EVERYONE))

    def halo_copy(index):
        dx, dy = AROUND[index]
        rows = {1: (BX[0] - HALO0, HALO0, 0), 0: (0, BX[0], HALO0), -1: (0, HALO0, BX[0] + HALO0)}[dx]
        cols = {1: (BY[0] - HALO0, HALO0, OY - HALO0), 0: (0, BY[0], OY), -1: (0, HALO0, OY + BY[0])}[dy]
        return pltpu.make_async_remote_copy(
            src_ref=density.at[rows[0] : rows[0] + rows[1], cols[0] : cols[0] + cols[1], :],
            dst_ref=b[0].at[rows[2] : rows[2] + rows[1], cols[2] : cols[2] + cols[1], :],
            send_sem=refs["halo_send"].at[index],
            recv_sem=refs["halo_recv"].at[index],
            device_id=device((dx, dy)),
            device_id_type=MESH,
        )

    halos = [halo_copy(index) for index in range(len(AROUND))]
    for copy in halos:
        copy.start()

    down(own[0], ownx[0], store_level(1), 0, -1, 34, 2)
    clip_x(own[1], 1, SPREAD[1], OY - 2, WIDE[0] // 2)
    presmooth(own[1], ownx[1], 1, 2, 4)
    down(own[1], ownx[1], store_level(2), 1, -2, 20, 2)
    clip_x(own[2], 2, SPREAD[2], OY - 2, WIDE[1] // 2)
    presmooth(own[2], ownx[2], 2, 3, 11)
    down(own[2], ownx[2], store_level(3), 2, -2, 12, 4)
    clip_x(own[3], 3, SPREAD[3], OY - 2, WIDE[2] // 2)
    presmooth(own[3], ownx[3], 3, 3, 14)

    def store_cells(coarse, both, size):
        for index in range(size):
            refs["cells4"][8 * index : 8 * index + 8, :] = both[index]

    down(own[3], ownx[3], store_cells, 3, -2, 8, 8)
    part = jnp.zeros((8, LANES), jnp.float32)
    for place in range(6):
        part = part + jnp.dot(
            refs["cells4"][pl.ds(place, 8, stride=8), :],
            packer[place * LANES : (place + 1) * LANES, :],
            precision=lax.Precision.HIGHEST,
            preferred_element_type=jnp.float32,
        )
    place_x = lax.broadcasted_iota(jnp.int32, (8, LANES), 0) - 2 + gx * BX[4]
    place_y = (lanes_of((8, LANES)) >> 3) - 2 + gy * BY[4]
    inside = (place_x >= 0) & (place_x < N * BX[4]) & (place_y >= 0) & (place_y < N * BY[4])
    part = jnp.where(inside, part, 0.0)
    refs["part4"][...] = part

    def line_copy(axis, step, slot):
        source, slots = (refs["part4"], refs["gathery"]) if axis == "gy" else (refs["strip"], refs["gatherx"])
        return pltpu.make_async_remote_copy(
            src_ref=source,
            dst_ref=slots.at[slot],
            send_sem=refs[axis + "_send"].at[step],
            recv_sem=refs[axis + "_recv"].at[slot],
            device_id=device((step, 0) if axis == "gx" else (0, step)),
            device_id_type=MESH,
        )

    sent = list(halos)
    for step in FAR_FIRST["gy"]:
        copy = line_copy("gy", step, gy)
        copy.start()
        sent.append(copy)

    parts = {}
    for index, (level, step) in enumerate([(k, d) for k in (3, 2, 1) for d in PARTNERS[k]]):
        low_x, many_x, _ = overlap(step[0], BX[level], SPREAD[level])
        low_y, many_y, _ = overlap(step[1], BY[level], SPREAD[level])
        copy = pltpu.make_async_remote_copy(
            src_ref=own[level].at[
                OX[level] + low_x : OX[level] + low_x + many_x, OY + low_y : OY + low_y + many_y, :
            ],
            dst_ref=inbox[level, step],
            send_sem=refs["part_send"].at[index],
            recv_sem=refs["part_recv"].at[index],
            device_id=device(step),
            device_id_type=MESH,
        )
        copy.start()
        parts[level, step] = copy
        sent.append(copy)

    def relax(field, out, level, weight, halo, size, scale=1.0, halves=None):
        scale_now = weight * 4.0**level / 6.0
        start, wide = START, WIDE[level]
        inside = inside_y(level, start, wide, scale)

        def body(row):
            center, total = around(field, row, size, level, start, wide)
            source = b[level][pl.ds(row, size), start : start + wide, :]
            result = ((1.0 - weight) * center + scale_now * source + (weight / 6.0) * total) * inside
            if halves is None:
                out[pl.ds(row, size), start : start + wide, :] = result
            else:
                first = row - OX[0] + 1
                halves[first // 33][pl.ds(first % 33, size)] = result

        chunks(OX[level] - halo, BX[level] + 2 * halo, size, body)
        if halves is None:
            clip_x(out, level, halo, start, wide)

    later.wait()
    for copy in halos:
        copy.wait_recv()
    clip_x(b[0], 0, HALO0, START, WIDE[0])
    for start in (0, 40):
        inside = inside_y(0, start, 8)

        def clip_y(row, start=start, inside=inside):
            b[0][pl.ds(row, 8), start : start + 8, :] *= inside
        chunks(0, 72, 8, clip_y)
    presmooth(b[0], x[0], 0, 3, 7)
    relax(x[0], f[0], 0, WEIGHT_FIRST, 2, 4)

    for step in range(1, N):
        slot = lax.rem(gy + N - step, N)
        line_copy("gy", step, slot).wait_recv()
    refs["gathery"][gy] = refs["part4"][...]
    lane = lanes_of((8, LANES))
    near = jnp.zeros((8, LANES), jnp.float32)
    far = jnp.zeros((8, LANES), jnp.float32)
    for slot in range(N):
        moved = pltpu.roll(refs["gathery"][slot], (16 * slot - 16) % LANES, 1)
        if slot < 7:
            near = near + moved
        elif slot > 8:
            far = far + moved
        else:
            low = jnp.where(lane >= 64, moved, 0.0)
            near = near + low
            far = far + (moved - low)
    refs["strip"][0:8, :] = near
    refs["strip"][8:16, :] = far
    for step in FAR_FIRST["gx"]:
        copy = line_copy("gx", step, gx)
        copy.start()
        sent.append(copy)

    relax(f[0], None, 0, WEIGHT_SECOND, 1, 11, FOUR_PI, (relaxed_low, relaxed_high))
    source_low[...] = FOUR_PI * b[0][4:36, 8:40, :]
    source_high[...] = FOUR_PI * b[0][36:68, 8:40, :]
    coarse_tables(refs["sines_x"], refs["sines_yz"], refs["gains"])

    for level in (3, 2, 1):
        spread = SPREAD[level]
        first_x, first_y = OX[level], OY
        rows = slice(first_x - spread, first_x + BX[level] + spread)
        cols = slice(first_y - spread, first_y + BY[level] + spread)
        b[level][rows, cols, :] = own[level][rows, cols, :]
        for step in PARTNERS[level]:
            parts[level, step].wait_recv()
            _, many_x, to_x = overlap(step[0], BX[level], spread)
            _, many_y, to_y = overlap(step[1], BY[level], spread)
            b[level][
                first_x + to_x : first_x + to_x + many_x, first_y + to_y : first_y + to_y + many_y, :
            ] += inbox[level, step][...]
        cover = BY[level] + 2 * HALO
        inside = inside_y(level, OY - HALO, cover)
        b[level][:, OY - HALO : OY - HALO + cover, :] *= inside
        clip_x(b[level], level, HALO, OY - HALO, cover)
        presmooth(b[level], x[level], level, 4, {3: 8, 2: 8, 1: 4}[level])

    for step in range(1, N):
        slot = lax.rem(gx + N - step, N)
        line_copy("gx", step, slot).wait_recv()
    refs["gatherx"][gx] = refs["strip"][...]
    b4 = refs["b4"]
    b4[...] = jnp.zeros((80, 256), jnp.float32)
    for slot in range(N):
        for tile in range(2):
            at = (slice(6 + 4 * slot, 14 + 4 * slot), slice(LANES * tile, LANES * tile + LANES))
            b4[at] += refs["gatherx"][slot, 8 * tile : 8 * tile + 8, :]

    def times(one, other):
        return jnp.dot(
            one, other, precision=lax.Precision.HIGHEST, preferred_element_type=jnp.float32
        )

    sines_yz = refs["sines_yz"][...]
    waves = times(refs["sines_x"][8:72, :64], b4[8:72, :])
    waves = times(waves, sines_yz) * refs["gains"][...]
    waves = times(refs["sines_x"][pl.ds(6 + 4 * gx, 8), :64], waves)
    coarsest = times(waves, sines_yz)

    lane = lanes_of((8, LANES))
    back = lax.rem(16 - 16 * gy + 2 * LANES, LANES)
    place = lane + 16 * gy - 16
    near = pltpu.roll(coarsest[:, :LANES], back, 1)
    far = pltpu.roll(coarsest[:, LANES:], back, 1)
    mine = jnp.where((place >= 0) & (place < LANES), near, 0.0)
    mine = jnp.where((place >= LANES) & (place < 2 * LANES), far, mine)
    wide4 = times(mine, spreader[...])
    for place in range(6):
        refs["e4wide"][pl.ds(place, 8, stride=8), :] = wide4[:, place * LANES : (place + 1) * LANES]

    def correct(level, first, count, size):
        half = 6 if level == 3 else WIDE[level] // 2

        def body(coarse):
            if level == 3:
                fix = refs["e4wide"][...].reshape(8, 8, LANES)[:, :half]
            else:
                fix = e[level + 1][pl.ds(OX[level + 1] + coarse, size), OY - 2 : OY - 2 + half, :]
            fix = jnp.broadcast_to(fix[:, None], (size, 2, half, LANES)).reshape(2 * size, half, LANES)
            row = OX[level] + 2 * coarse
            for parity in range(2):
                place = (pl.ds(row, 2 * size), pl.ds(START + parity, half, stride=2), slice(None))
                x[level][place] = x[level][place] + fix
        chunks(first, count, size, body)

    correct(3, -2, 8, 8)
    relax(x[3], f[3], 3, WEIGHT_FIRST, 3, 14)
    relax(f[3], e[3], 3, WEIGHT_SECOND, 2, 12)
    correct(2, -2, 12, 6)
    relax(x[2], f[2], 2, WEIGHT_FIRST, 3, 11)
    relax(f[2], e[2], 2, WEIGHT_SECOND, 2, 10)
    correct(1, -2, 20, 4)
    relax(x[1], f[1], 1, WEIGHT_FIRST, 4, 4)
    relax(f[1], e[1], 1, WEIGHT_SECOND, 2, 4)

    for copy in sent:
        copy.wait_send()


def finish(
    e1, relaxed_low, relaxed_high, source_low, source_high, potential, residual, first, pot, out, out_sem
):
    relaxed = (relaxed_low, relaxed_high)
    source = (source_low, source_high)

    inside = inside_y(1, OY - 1, 18, FOUR_PI)

    def spread(coarse):
        rows = pl.ds(OX[1] + coarse, 17)
        cells = e1[rows, OY - 1 : OY + 17, :]
        same = (1.0 - WEIGHT_FIRST * 2.0 / 3.0) * cells + (WEIGHT_FIRST / 6.0) * along_z(cells, 0)
        same = same * inside
        share = inside * (WEIGHT_FIRST / 6.0)
        for odd_x in range(2):
            beside = e1[pl.ds(OX[1] + coarse + 2 * odd_x - 1, 17), OY - 1 : OY + 17, :]
            for odd_y in range(2):
                below = OY - 2 + 2 * odd_y
                both = beside + e1[rows, below : below + 18, :]
                both = same + share * both
                for index in range(17):
                    row = OX[0] + 2 * (coarse + index) + odd_x
                    first[row, pl.ds(OY - 2 + odd_y, 18, stride=2), :] = both[index]

    chunks(-1, 34, 17, spread)
    clip_x(first, 0, 2, START, WIDE[0])

    inside = inside_y(0, START, WIDE[0])
    cols = slice(START, START + WIDE[0])

    def second(row):
        center, total = around(first, row, 11, 0, START, WIDE[0])
        later = (1.0 - WEIGHT_SECOND) * center + (WEIGHT_SECOND / 6.0) * total
        place = row - OX[0] + 1
        pot[pl.ds(row, 11), cols, :] = (
            relaxed[place // 33][pl.ds(place % 33, 11)] + later * inside
        )

    chunks(OX[0] - 1, BX[0] + 2, 11, second)
    clip_x(pot, 0, 1, START, WIDE[0])

    stores = []

    def store(origin, target, index, part):
        copy = pltpu.make_async_copy(
            origin, target.at[16 * part : 16 * part + 16], out_sem.at[index, part]
        )
        copy.start()
        stores.append(copy)

    for part in range(4):
        store(pot.at[4 + 16 * part : 20 + 16 * part, OY : OY + BY[0], :], potential, 0, part)

    def rest(row):
        center, total = around(pot, row, 8, 0, OY, BY[0])
        place = row - OX[0]
        out[pl.ds(place, 8)] = source[place // 32][pl.ds(place % 32, 8)] - 6.0 * center + total

    for part in range(4):
        chunks(4 + 16 * part, 16, 8, rest)
        store(out.at[16 * part : 16 * part + 16], residual, 1, part)
    for copy in stores:
        copy.wait()


def on_device(density):
    def cells(*shape):
        return pltpu.VMEM(shape + (LANES,), jnp.float32)

    level_arrays = [cells(ROWS[k], COLS[k]) for k in range(4)]
    dma = pltpu.SemaphoreType.DMA
    scratch = level_arrays * 6 + [
        cells(34, 40),
        cells(768),
        pltpu.VMEM((LANES, 768), jnp.float32),
        cells(64),
        cells(8),
        cells(N, 8),
        cells(16),
        cells(N, 16),
        pltpu.VMEM((80, 256), jnp.float32),
        cells(64),
        cells(80),
        pltpu.VMEM((256, 256), jnp.float32),
        pltpu.VMEM((64, 256), jnp.float32),
        dma((5,)),
        dma((8,)),
        dma((8,)),
        dma((30,)),
        dma((30,)),
        dma((N,)),
        dma((N,)),
        dma((N,)),
        dma((N,)),
    ]
    for level in (1, 2, 3):
        for step in PARTNERS[level]:
            many_x = overlap(step[0], BX[level], SPREAD[level])[1]
            many_y = overlap(step[1], BY[level], SPREAD[level])[1]
            scratch.append(cells(many_x, many_y))
    hbm = pl.BlockSpec(memory_space=pltpu.HBM)
    vmem = pl.BlockSpec(memory_space=pltpu.VMEM)
    shapes = [(ROWS[1], COLS[1])] + [(33, WIDE[0])] * 2 + [(32, 32)] * 2
    shared = pl.pallas_call(
        kernel,
        out_shape=[jax.ShapeDtypeStruct(shape + (LANES,), jnp.float32) for shape in shapes],
        in_specs=[hbm],
        out_specs=[vmem] * 5,
        scratch_shapes=scratch,
        compiler_params=pltpu.CompilerParams(
            collective_id=0, has_side_effects=True, vmem_limit_bytes=50 * 2**20 + 2**18
        ),
        name="vcycle",
    )(density)
    return pl.pallas_call(
        finish,
        out_shape=[jax.ShapeDtypeStruct(density.shape, jnp.float32)] * 2,
        in_specs=[vmem] * 5,
        out_specs=[hbm] * 2,
        scratch_shapes=[
            cells(ROWS[0], COLS[0]),
            cells(ROWS[0], COLS[0]),
            cells(64, 32),
            dma((2, 4)),
        ],
        compiler_params=pltpu.CompilerParams(vmem_limit_bytes=24 * 2**20),
        name="finish",
    )(*shared)


def solution(mesh):
    return jax.shard_map(
        on_device,
        mesh=mesh,
        in_specs=(P("gx", "gy", None),),
        out_specs=(P("gx", "gy", None), P("gx", "gy", None)),
        check_vma=False,
    )
```

```python
import math

import jax
import jax.numpy as jnp
from jax import lax
from jax.experimental import pallas as pl
from jax.experimental.pallas import tpu as pltpu
from jax.sharding import PartitionSpec as P

LEVELS = 4
JACOBI = 20
FOUR_PI = 4.0 * math.pi
WEIGHT_FIRST = 1.0 / (1.25 + 0.75 * math.cos(math.pi / 4.0))
WEIGHT_SECOND = 1.0 / (1.25 - 0.75 * math.cos(math.pi / 4.0))
JACOBI_WEIGHT = 0.8

N = 16
LANES = 128
BX = (64, 32, 16, 8, 4)
BY = (32, 16, 8, 4, 2)
OX = (4, 6, 6, 6)
OY = 8
ROWS = (72, 44, 28, 20)
COLS = (48, 32, 24, 24)
START = 4
WIDE = (40, 24, 16, 16)
SPREAD = (0, 1, 2, 2)
HALO = 5
GROUP = (1, 2, 4, 4)
HALO0 = 4
MESH = pl.DeviceIdType.MESH

AROUND = [(dx, dy) for dx in (-1, 0, 1) for dy in (-1, 0, 1) if (dx, dy) != (0, 0)]
AROUND3 = [(dx, dy) for dx in (-1, 0, 1) for dy in (-2, -1, 0, 1, 2) if (dx, dy) != (0, 0)]
PARTNERS = {1: AROUND, 2: AROUND, 3: AROUND3}
EVERYONE = sorted(
    {(dx % N, dy % N) for dx, dy in AROUND3}
    | {(d, 0) for d in range(1, N)}
    | {(0, d) for d in range(1, N)}
)

KINDS = ["own", "ownx", "b", "x", "f", "e"]
SINGLE = [
    "pairs",
    "packer",
    "spreader",
    "cells4",
    "part4",
    "gathery",
    "strip",
    "gatherx",
    "b4",
    "e4wide",
    "sines_x",
    "sines_yz",
    "gains",
    "packed1",
    "packed2",
    "packed3",
    "load_sem",
    "halo_send",
    "halo_recv",
    "part_send",
    "part_recv",
    "gy_send",
    "gy_recv",
    "gx_send",
    "gx_recv",
]


def sine_table(row, col, count):
    period = 2.0 * (count + 1)
    turns = (row + 1.0) * (col + 1.0)
    turns = turns - period * jnp.floor((turns + 0.5) * (1.0 / period))
    turns = turns - (count + 1.0)
    size = jnp.abs(turns)
    size = jnp.minimum(size, (count + 1.0) - size)
    angle = size * (math.pi / (count + 1))
    square = angle * angle
    total = 1.0
    for order in (12, 10, 8, 6, 4, 2):
        total = 1.0 - total * square * (1.0 / (order * (order + 1)))
    value = angle * total * math.sqrt(2.0 / (count + 1))
    return jnp.where(turns < 0.0, value, -value)


def coarse_tables(sines_x, sines_yz, gains):
    def places(shape):
        return [lax.broadcasted_iota(jnp.int32, shape, axis) for axis in range(2)]

    def real(numbers):
        return numbers.astype(jnp.float32)

    row, col = places((80, LANES))
    inside = (row >= 8) & (row < 72) & (col < 64)
    sines_x[...] = jnp.where(inside, sine_table(real(row - 8), real(col), 64), 0.0)
    for tile in range(8):
        row, col = places((32, 256))
        row = row + 32 * tile
        sines_yz[32 * tile : 32 * tile + 32, :] = sine_table(
            real(row >> 3), real(col >> 3), 32
        ) * sine_table(real(row & 7), real(col & 7), 8)

    def value(place, count):
        sine = sine_table(real(place), jnp.zeros(place.shape, jnp.float32), 2 * count + 1)
        return (4.0 * (count + 1)) * sine * sine

    row, col = places((64, 256))
    damped = (JACOBI_WEIGHT / 6.0) * (value(row, 64) + value(col >> 3, 32) + value(col & 7, 8))
    kept = 1.0 - damped
    power = kept * kept
    power = power * power
    fourth = power
    power = power * power
    power = power * power * fourth
    assert JACOBI == 20
    gains[...] = (JACOBI_WEIGHT * 4.0**LEVELS / 6.0) * (1.0 - power) / damped


def ring(step, count):
    return min(step % count, -step % count)


def hops_x(step):
    return sum(ring((core + step) // 2 - core // 2, 8) for core in range(2))


def hops_y(step):
    return sum(ring((x + step) // 4, 4) + ring((x + step) % 4 - x, 4) for x in range(4))


FAR_FIRST = {
    "gx": sorted(range(1, N), key=hops_x, reverse=True),
    "gy": sorted(range(1, N), key=hops_y, reverse=True),
}


def overlap(step, block, spread):
    low = max(-spread, step * block - HALO)
    high = min(block + spread, step * block + block + HALO)
    return low, high - low, low - step * block


def groups(step, level):
    low, many, _ = overlap(step, BX[level], SPREAD[level])
    low += SPREAD[level]
    first = low // GROUP[level]
    last = -(-(low + many) // GROUP[level])
    return first, last - first, low - first * GROUP[level]


def lanes_of(shape):
    return lax.broadcasted_iota(jnp.int32, shape, len(shape) - 1)


def along_z(cells, level):
    step = 1 << level
    axis = cells.ndim - 1
    lane = lanes_of(cells.shape)
    below = jnp.where(lane >= step, pltpu.roll(cells, step, axis), 0.0)
    above = jnp.where(lane < LANES - step, pltpu.roll(cells, LANES - step, axis), 0.0)
    return below + above


def pair_z(cells, level):
    step = 1 << level
    axis = cells.ndim - 1
    odd = (lanes_of(cells.shape) >> level) & 1
    other = jnp.where(odd == 0, pltpu.roll(cells, LANES - step, axis), pltpu.roll(cells, step, axis))
    return cells + other


def pack(rows, size):
    count, wide = rows.shape[0] // size, rows.shape[1]
    rows = rows.reshape(count, size, wide, LANES)
    which = lanes_of((count, wide, LANES)) & (size - 1)
    packed = rows[:, size - 1]
    for index in range(size - 1):
        packed = jnp.where(which == index, rows[:, index], packed)
    return packed


def unpack(packed, size):
    lane = lanes_of(packed.shape)
    rows = [packed]
    bit = 1
    while bit < size:
        even = [jnp.where((lane & bit) == 0, row, pltpu.roll(row, bit, 2)) for row in rows]
        odd = [jnp.where((lane & bit) == 0, pltpu.roll(row, LANES - bit, 2), row) for row in rows]
        rows = even + odd
        bit *= 2
    return jnp.stack(rows, axis=1).reshape(size * packed.shape[0], packed.shape[1], LANES)


def around(ref, row, count, level, start, wide):
    tall = ref[pl.ds(row - 1, count + 2), start : start + wide, :]
    center = tall[1 : count + 1]
    total = tall[:count] + tall[2:]
    total = total + ref[pl.ds(row, count), start - 1 : start - 1 + wide, :]
    total = total + ref[pl.ds(row, count), start + 1 : start + 1 + wide, :]
    return center, total + along_z(center, level)


def inside_y(level, start, wide, scale=1.0):
    place = lax.broadcasted_iota(jnp.int32, (wide, LANES), 0) + (start - OY)
    place = place + lax.axis_index("gy") * BY[level]
    return jnp.where((place >= 0) & (place < N * BY[level]), scale, 0.0)


def clip_x(ref, level, halo, start, wide):
    gx = lax.axis_index("gx")
    first = OX[level]
    last = first + BX[level]
    ref[first - halo : first, start : start + wide, :] *= jnp.where(gx > 0, 1.0, 0.0)
    ref[last : last + halo, start : start + wide, :] *= jnp.where(gx < N - 1, 1.0, 0.0)


def chunks(first, count, size, body):
    assert count % size == 0
    for index in range(count // size):
        body(first + index * size)


def kernel(density, e1_out, relaxed_low, relaxed_high, source_low, source_high, *scratch):
    names = [kind + str(level) for kind in KINDS for level in range(LEVELS)] + SINGLE
    refs = dict(zip(names, scratch))
    inbox = dict(zip([(k, d) for k in (1, 2, 3) for d in PARTNERS[k]], scratch[len(names) :]))
    own = [refs[f"own{k}"] for k in range(4)]
    ownx = [refs[f"ownx{k}"] for k in range(4)]
    b = [refs[f"b{k}"] for k in range(4)]
    x = [refs[f"x{k}"] for k in range(4)]
    f = [refs[f"f{k}"] for k in range(4)]
    e = [None, e1_out, refs["e2"], refs["e3"]]
    pairs, packer, spreader = refs["pairs"], refs["packer"], refs["spreader"]

    gx, gy = lax.axis_index("gx"), lax.axis_index("gy")

    def device(step):
        return {"gx": lax.rem(gx + step[0] + N, N), "gy": lax.rem(gy + step[1] + N, N)}

    barrier = pltpu.get_barrier_semaphore()
    for step in EVERYONE:
        pl.semaphore_signal(barrier, inc=1, device_id=device(step), device_id_type=MESH)

    loads = [
        pltpu.make_async_copy(
            density.at[16 * part : 16 * part + 16],
            own[0].at[4 + 16 * part : 20 + 16 * part, 8:40, :],
            refs["load_sem"].at[part],
        )
        for part in range(4)
    ]
    for copy in loads:
        copy.start()

    def zero(ref, rows, cols):
        ref[rows[0] : rows[1], cols[0] : cols[1], :] = jnp.zeros(
            (rows[1] - rows[0], cols[1] - cols[0], LANES), jnp.float32
        )

    for ref in (own[0], ownx[0]):
        zero(ref, (0, 4), (0, 48))
        zero(ref, (68, 72), (0, 48))
        zero(ref, (4, 68), (0, 8))
        zero(ref, (4, 68), (40, 48))
    for level in (1, 2, 3):
        zero(own[level], (0, ROWS[level]), (0, COLS[level]))
        zero(ownx[level], (0, ROWS[level]), (0, COLS[level]))
        zero(b[level], (0, ROWS[level]), (0, COLS[level]))
    row = lax.broadcasted_iota(jnp.int32, (768, LANES), 0)
    col = lax.broadcasted_iota(jnp.int32, (768, LANES), 1)
    hit = ((row & 7) == 0) & (((row >> 4) & 7) == (col & 7)) & ((row >> 7) == (col >> 3))
    packer[...] = jnp.where(hit, 0.125, 0.0)
    row = lax.broadcasted_iota(jnp.int32, (LANES, 768), 0)
    col = lax.broadcasted_iota(jnp.int32, (LANES, 768), 1)
    hit = ((row >> 3) == (col >> 7)) & ((row & 7) == ((col >> 4) & 7))
    spreader[...] = jnp.where(hit, 1.0, 0.0)

    def presmooth(source, out, level, halo, size, ready=None):
        inverse = 0.25**level
        scale_first = WEIGHT_FIRST * 4.0**level / 6.0
        scale_second = WEIGHT_SECOND * 4.0**level / 6.0
        linear = scale_first + scale_second
        mixed = scale_first * scale_second * inverse
        start, wide = START, WIDE[level]
        inside = inside_y(level, start, wide)

        def body(row):
            if ready is not None:
                ready(row + size)
            center, total = around(source, row, size, level, start, wide)
            out[pl.ds(row, size), start : start + wide, :] = (
                (linear - 6.0 * mixed) * center + mixed * total
            ) * inside
        chunks(OX[level] - halo, BX[level] + 2 * halo, size, body)
        clip_x(out, level, halo, start, wide)

    def down(source, field, out, level, first, count, size):
        inverse = 0.25**level
        start, wide = START, WIDE[level]
        half = wide // 2

        def body(coarse):
            row = OX[level] + 2 * coarse
            center, total = around(field, row, 2 * size, level, start, wide)
            rest = source[pl.ds(row, 2 * size), start : start + wide, :] - inverse * (6.0 * center - total)
            rest = rest.reshape(size, 2, wide, LANES)
            at = pl.ds(coarse - first, size)
            pairs[at, :wide, :] = rest[:, 0] + rest[:, 1]
            both = pairs[at, pl.ds(0, half, stride=2), :] + pairs[at, pl.ds(1, half, stride=2), :]
            out(coarse, both, size)

        chunks(first, count, size, body)

    def store_level(level):
        start, wide = OY - 2, WIDE[level - 1] // 2
        inside = inside_y(level, start, wide)

        def out(coarse, both, size):
            own[level][pl.ds(OX[level] + coarse, size), start : start + wide, :] = (
                0.125 * pair_z(both, level - 1) * inside
            )
        return out

    waiting = list(loads)

    def loaded(row):
        while waiting and (row >= 4 + 16 * (4 - len(waiting)) or row >= 67):
            waiting.pop(0).wait()

    presmooth(own[0], ownx[0], 0, 1, 11, loaded)

    def halo_copy(index):
        dx, dy = AROUND[index]
        rows = {1: (BX[0] - HALO0, HALO0, 0), 0: (0, BX[0], HALO0), -1: (0, HALO0, BX[0] + HALO0)}[dx]
        cols = {1: (BY[0] - HALO0, HALO0, OY - HALO0), 0: (0, BY[0], OY), -1: (0, HALO0, OY + BY[0])}[dy]
        return pltpu.make_async_remote_copy(
            src_ref=own[0].at[
                4 + rows[0] : 4 + rows[0] + rows[1], OY + cols[0] : OY + cols[0] + cols[1], :
            ],
            dst_ref=b[0].at[rows[2] : rows[2] + rows[1], cols[2] : cols[2] + cols[1], :],
            send_sem=refs["halo_send"].at[index],
            recv_sem=refs["halo_recv"].at[index],
            device_id=device((dx, dy)),
            device_id_type=MESH,
        )

    halos = [halo_copy(index) for index in range(len(AROUND))]
    pl.semaphore_wait(barrier, len(EVERYONE))
    for copy in halos:
        copy.start()
    down(own[0], ownx[0], store_level(1), 0, -1, 34, 2)
    clip_x(own[1], 1, SPREAD[1], OY - 2, WIDE[0] // 2)
    presmooth(own[1], ownx[1], 1, 2, 4)
    down(own[1], ownx[1], store_level(2), 1, -2, 20, 2)
    clip_x(own[2], 2, SPREAD[2], OY - 2, WIDE[1] // 2)
    presmooth(own[2], ownx[2], 2, 3, 11)
    down(own[2], ownx[2], store_level(3), 2, -2, 12, 4)
    clip_x(own[3], 3, SPREAD[3], OY - 2, WIDE[2] // 2)
    presmooth(own[3], ownx[3], 3, 3, 14)

    def store_cells(coarse, both, size):
        for index in range(size):
            refs["cells4"][8 * index : 8 * index + 8, :] = both[index]

    down(own[3], ownx[3], store_cells, 3, -2, 8, 8)
    part = jnp.zeros((8, LANES), jnp.float32)
    for place in range(6):
        part = part + jnp.dot(
            refs["cells4"][pl.ds(place, 8, stride=8), :],
            packer[place * LANES : (place + 1) * LANES, :],
            precision=lax.Precision.HIGHEST,
            preferred_element_type=jnp.float32,
        )
    place_x = lax.broadcasted_iota(jnp.int32, (8, LANES), 0) - 2 + gx * BX[4]
    place_y = (lanes_of((8, LANES)) >> 3) - 2 + gy * BY[4]
    inside = (place_x >= 0) & (place_x < N * BX[4]) & (place_y >= 0) & (place_y < N * BY[4])
    part = jnp.where(inside, part, 0.0)
    refs["part4"][...] = part

    def line_copy(axis, step, slot):
        source, slots = (refs["part4"], refs["gathery"]) if axis == "gy" else (refs["strip"], refs["gatherx"])
        return pltpu.make_async_remote_copy(
            src_ref=source,
            dst_ref=slots.at[slot],
            send_sem=refs[axis + "_send"].at[step],
            recv_sem=refs[axis + "_recv"].at[slot],
            device_id=device((step, 0) if axis == "gx" else (0, step)),
            device_id_type=MESH,
        )

    sent = list(halos)
    for step in FAR_FIRST["gy"]:
        copy = line_copy("gy", step, gy)
        copy.start()
        sent.append(copy)

    parts = {}
    for level in (3, 2, 1):
        spread = SPREAD[level]
        first = OX[level] - spread
        wide = BY[level] + 2 * spread
        packed = refs["packed" + str(level)]
        packed[:, OY : OY + wide, :] = pack(
            own[level][first : first + BX[level] + 2 * spread, OY - spread : OY - spread + wide, :],
            GROUP[level],
        )
        for step in PARTNERS[level]:
            index = len(parts)
            first, count, _ = groups(step[0], level)
            low_y, many_y, _ = overlap(step[1], BY[level], spread)
            low_y += OY + spread
            copy = pltpu.make_async_remote_copy(
                src_ref=packed.at[first : first + count, low_y : low_y + many_y, :],
                dst_ref=inbox[level, step],
                send_sem=refs["part_send"].at[index],
                recv_sem=refs["part_recv"].at[index],
                device_id=device(step),
                device_id_type=MESH,
            )
            copy.start()
            parts[level, step] = copy
            sent.append(copy)

    def relax(field, out, level, weight, halo, size, scale=1.0, halves=None):
        scale_now = weight * 4.0**level / 6.0
        start, wide = START, WIDE[level]
        inside = inside_y(level, start, wide, scale)

        def body(row):
            center, total = around(field, row, size, level, start, wide)
            source = b[level][pl.ds(row, size), start : start + wide, :]
            result = ((1.0 - weight) * center + scale_now * source + (weight / 6.0) * total) * inside
            if halves is None:
                out[pl.ds(row, size), start : start + wide, :] = result
            else:
                first = row - OX[0] + 1
                halves[first // 33][pl.ds(first % 33, size)] = result

        chunks(OX[level] - halo, BX[level] + 2 * halo, size, body)
        if halves is None:
            clip_x(out, level, halo, start, wide)

    coarse_tables(refs["sines_x"], refs["sines_yz"], refs["gains"])
    b[0][4:68, 8:40, :] = own[0][4:68, 8:40, :]
    for copy in halos:
        copy.wait_recv()
    clip_x(b[0], 0, HALO0, START, WIDE[0])
    for start in (0, 40):
        inside = inside_y(0, start, 8)

        def clip_y(row, start=start, inside=inside):
            b[0][pl.ds(row, 8), start : start + 8, :] *= inside
        chunks(0, 72, 8, clip_y)
    presmooth(b[0], x[0], 0, 3, 7)

    for step in range(1, N):
        slot = lax.rem(gy + N - step, N)
        line_copy("gy", step, slot).wait_recv()
    refs["gathery"][gy] = refs["part4"][...]
    lane = lanes_of((8, LANES))
    near = jnp.zeros((8, LANES), jnp.float32)
    far = jnp.zeros((8, LANES), jnp.float32)
    for slot in range(N):
        moved = pltpu.roll(refs["gathery"][slot], (16 * slot - 16) % LANES, 1)
        if slot < 7:
            near = near + moved
        elif slot > 8:
            far = far + moved
        else:
            low = jnp.where(lane >= 64, moved, 0.0)
            near = near + low
            far = far + (moved - low)
    refs["strip"][0:8, :] = near
    refs["strip"][8:16, :] = far
    for step in FAR_FIRST["gx"]:
        copy = line_copy("gx", step, gx)
        copy.start()
        sent.append(copy)

    relax(x[0], f[0], 0, WEIGHT_FIRST, 2, 4)
    relax(f[0], None, 0, WEIGHT_SECOND, 1, 11, FOUR_PI, (relaxed_low, relaxed_high))
    source_low[...] = FOUR_PI * b[0][4:36, 8:40, :]
    source_high[...] = FOUR_PI * b[0][36:68, 8:40, :]

    for level in (3, 2, 1):
        spread = SPREAD[level]
        first_x, first_y = OX[level], OY
        rows = slice(first_x - spread, first_x + BX[level] + spread)
        cols = slice(first_y - spread, first_y + BY[level] + spread)
        b[level][rows, cols, :] = own[level][rows, cols, :]
        for step in PARTNERS[level]:
            parts[level, step].wait_recv()
            _, many_x, to_x = overlap(step[0], BX[level], spread)
            _, many_y, to_y = overlap(step[1], BY[level], spread)
            skip = groups(step[0], level)[2]
            rows = unpack(inbox[level, step][...], GROUP[level])
            b[level][
                first_x + to_x : first_x + to_x + many_x, first_y + to_y : first_y + to_y + many_y, :
            ] += rows[skip : skip + many_x]
        cover = BY[level] + 2 * HALO
        inside = inside_y(level, OY - HALO, cover)
        b[level][:, OY - HALO : OY - HALO + cover, :] *= inside
        clip_x(b[level], level, HALO, OY - HALO, cover)
        presmooth(b[level], x[level], level, 4, {3: 8, 2: 8, 1: 4}[level])

    for step in range(1, N):
        slot = lax.rem(gx + N - step, N)
        line_copy("gx", step, slot).wait_recv()
    refs["gatherx"][gx] = refs["strip"][...]
    b4 = refs["b4"]
    b4[...] = jnp.zeros((80, 256), jnp.float32)
    for slot in range(N):
        for tile in range(2):
            at = (slice(6 + 4 * slot, 14 + 4 * slot), slice(LANES * tile, LANES * tile + LANES))
            b4[at] += refs["gatherx"][slot, 8 * tile : 8 * tile + 8, :]

    def times(one, other):
        return jnp.dot(
            one, other, precision=lax.Precision.HIGHEST, preferred_element_type=jnp.float32
        )

    sines_yz = refs["sines_yz"][...]
    waves = times(refs["sines_x"][8:72, :64], b4[8:72, :])
    waves = times(waves, sines_yz) * refs["gains"][...]
    waves = times(refs["sines_x"][pl.ds(6 + 4 * gx, 8), :64], waves)
    coarsest = times(waves, sines_yz)

    lane = lanes_of((8, LANES))
    back = lax.rem(16 - 16 * gy + 2 * LANES, LANES)
    place = lane + 16 * gy - 16
    near = pltpu.roll(coarsest[:, :LANES], back, 1)
    far = pltpu.roll(coarsest[:, LANES:], back, 1)
    mine = jnp.where((place >= 0) & (place < LANES), near, 0.0)
    mine = jnp.where((place >= LANES) & (place < 2 * LANES), far, mine)
    wide4 = times(mine, spreader[...])
    for place in range(6):
        refs["e4wide"][pl.ds(place, 8, stride=8), :] = wide4[:, place * LANES : (place + 1) * LANES]

    def correct(level, first, count, size):
        half = 6 if level == 3 else WIDE[level] // 2

        def body(coarse):
            if level == 3:
                fix = refs["e4wide"][...].reshape(8, 8, LANES)[:, :half]
            else:
                fix = e[level + 1][pl.ds(OX[level + 1] + coarse, size), OY - 2 : OY - 2 + half, :]
            fix = jnp.broadcast_to(fix[:, None], (size, 2, half, LANES)).reshape(2 * size, half, LANES)
            row = OX[level] + 2 * coarse
            for parity in range(2):
                place = (pl.ds(row, 2 * size), pl.ds(START + parity, half, stride=2), slice(None))
                x[level][place] = x[level][place] + fix
        chunks(first, count, size, body)

    correct(3, -2, 8, 8)
    relax(x[3], f[3], 3, WEIGHT_FIRST, 3, 14)
    relax(f[3], e[3], 3, WEIGHT_SECOND, 2, 12)
    correct(2, -2, 12, 6)
    relax(x[2], f[2], 2, WEIGHT_FIRST, 3, 11)
    relax(f[2], e[2], 2, WEIGHT_SECOND, 2, 10)
    correct(1, -2, 20, 4)
    relax(x[1], f[1], 1, WEIGHT_FIRST, 4, 4)
    relax(f[1], e[1], 1, WEIGHT_SECOND, 2, 4)

    for copy in sent:
        copy.wait_send()


def finish(
    e1, relaxed_low, relaxed_high, source_low, source_high, potential, residual, first, pot, out, out_sem
):
    relaxed = (relaxed_low, relaxed_high)
    source = (source_low, source_high)

    inside = inside_y(1, OY - 1, 18, FOUR_PI)

    def spread(coarse):
        rows = pl.ds(OX[1] + coarse, 17)
        cells = e1[rows, OY - 1 : OY + 17, :]
        same = (1.0 - WEIGHT_FIRST * 2.0 / 3.0) * cells + (WEIGHT_FIRST / 6.0) * along_z(cells, 0)
        same = same * inside
        share = inside * (WEIGHT_FIRST / 6.0)
        for odd_x in range(2):
            beside = e1[pl.ds(OX[1] + coarse + 2 * odd_x - 1, 17), OY - 1 : OY + 17, :]
            for odd_y in range(2):
                below = OY - 2 + 2 * odd_y
                both = beside + e1[rows, below : below + 18, :]
                both = same + share * both
                for index in range(17):
                    row = OX[0] + 2 * (coarse + index) + odd_x
                    first[row, pl.ds(OY - 2 + odd_y, 18, stride=2), :] = both[index]

    chunks(-1, 34, 17, spread)
    clip_x(first, 0, 2, START, WIDE[0])

    inside = inside_y(0, START, WIDE[0])
    cols = slice(START, START + WIDE[0])

    def second(row):
        center, total = around(first, row, 11, 0, START, WIDE[0])
        later = (1.0 - WEIGHT_SECOND) * center + (WEIGHT_SECOND / 6.0) * total
        place = row - OX[0] + 1
        pot[pl.ds(row, 11), cols, :] = (
            relaxed[place // 33][pl.ds(place % 33, 11)] + later * inside
        )

    chunks(OX[0] - 1, BX[0] + 2, 11, second)
    clip_x(pot, 0, 1, START, WIDE[0])

    stores = []

    def store(origin, target, index, part):
        copy = pltpu.make_async_copy(
            origin, target.at[16 * part : 16 * part + 16], out_sem.at[index, part]
        )
        copy.start()
        stores.append(copy)

    for part in range(4):
        store(pot.at[4 + 16 * part : 20 + 16 * part, OY : OY + BY[0], :], potential, 0, part)

    def rest(row):
        center, total = around(pot, row, 8, 0, OY, BY[0])
        place = row - OX[0]
        out[pl.ds(place, 8)] = source[place // 32][pl.ds(place % 32, 8)] - 6.0 * center + total

    for part in range(4):
        chunks(4 + 16 * part, 16, 8, rest)
        store(out.at[16 * part : 16 * part + 16], residual, 1, part)
    for copy in stores:
        copy.wait()


def on_device(density):
    def cells(*shape):
        return pltpu.VMEM(shape + (LANES,), jnp.float32)

    level_arrays = [cells(ROWS[k], COLS[k]) for k in range(4)]
    dma = pltpu.SemaphoreType.DMA
    scratch = level_arrays * 6 + [
        cells(34, 40),
        cells(768),
        pltpu.VMEM((LANES, 768), jnp.float32),
        cells(64),
        cells(8),
        cells(N, 8),
        cells(16),
        cells(N, 16),
        pltpu.VMEM((80, 256), jnp.float32),
        cells(64),
        cells(80),
        pltpu.VMEM((256, 256), jnp.float32),
        pltpu.VMEM((64, 256), jnp.float32),
        cells(17, 32),
        cells(5, 24),
        cells(3, 24),
        dma((4,)),
        dma((8,)),
        dma((8,)),
        dma((30,)),
        dma((30,)),
        dma((N,)),
        dma((N,)),
        dma((N,)),
        dma((N,)),
    ]
    for level in (1, 2, 3):
        for step in PARTNERS[level]:
            many_y = overlap(step[1], BY[level], SPREAD[level])[1]
            scratch.append(cells(groups(step[0], level)[1], many_y))
    hbm = pl.BlockSpec(memory_space=pltpu.HBM)
    vmem = pl.BlockSpec(memory_space=pltpu.VMEM)
    shapes = [(ROWS[1], COLS[1])] + [(33, WIDE[0])] * 2 + [(32, 32)] * 2
    shared = pl.pallas_call(
        kernel,
        out_shape=[jax.ShapeDtypeStruct(shape + (LANES,), jnp.float32) for shape in shapes],
        in_specs=[hbm],
        out_specs=[vmem] * 5,
        scratch_shapes=scratch,
        compiler_params=pltpu.CompilerParams(
            collective_id=0, has_side_effects=True, vmem_limit_bytes=50 * 2**20 + 2**18
        ),
        name="vcycle",
    )(density)
    return pl.pallas_call(
        finish,
        out_shape=[jax.ShapeDtypeStruct(density.shape, jnp.float32)] * 2,
        in_specs=[vmem] * 5,
        out_specs=[hbm] * 2,
        scratch_shapes=[
            cells(ROWS[0], COLS[0]),
            cells(ROWS[0], COLS[0]),
            cells(64, 32),
            dma((2, 4)),
        ],
        compiler_params=pltpu.CompilerParams(vmem_limit_bytes=24 * 2**20),
        name="finish",
    )(*shared)


def solution(mesh):
    return jax.shard_map(
        on_device,
        mesh=mesh,
        in_specs=(P("gx", "gy", None),),
        out_specs=(P("gx", "gy", None), P("gx", "gy", None)),
        check_vma=False,
    )
```

```python
import math

import jax
import jax.numpy as jnp
from jax import lax
from jax.experimental import pallas as pl
from jax.experimental.pallas import tpu as pltpu
from jax.sharding import PartitionSpec as P

LEVELS = 4
JACOBI = 20
FOUR_PI = 4.0 * math.pi
WEIGHT_FIRST = 1.0 / (1.25 + 0.75 * math.cos(math.pi / 4.0))
WEIGHT_SECOND = 1.0 / (1.25 - 0.75 * math.cos(math.pi / 4.0))
JACOBI_WEIGHT = 0.8

N = 16
LANES = 128
BX = (64, 32, 16, 8, 4)
BY = (32, 16, 8, 4, 2)
OX = (4, 6, 6, 6)
OY = 8
ROWS = (72, 44, 28, 20)
COLS = (48, 32, 24, 24)
START = 4
WIDE = (40, 24, 16, 16)
SPREAD = (0, 1, 2, 2)
HALO = 5
GROUP = (1, 2, 4, 4)
SPREAD0 = 3
MESH = pl.DeviceIdType.MESH

AROUND = [(dx, dy) for dx in (-1, 0, 1) for dy in (-1, 0, 1) if (dx, dy) != (0, 0)]
AROUND3 = [(dx, dy) for dx in (-1, 0, 1) for dy in (-2, -1, 0, 1, 2) if (dx, dy) != (0, 0)]
PARTNERS = {0: AROUND, 1: AROUND, 2: AROUND, 3: AROUND3}
EVERYONE = sorted(
    {(dx % N, dy % N) for dx, dy in AROUND3}
    | {(d, 0) for d in range(1, N)}
    | {(0, d) for d in range(1, N)}
)

KINDS = ["own", "ownx", "b", "x", "f", "e"]
SINGLE = [
    "pairs",
    "packer",
    "spreader",
    "cells4",
    "part4",
    "gathery",
    "strip",
    "gatherx",
    "b4",
    "e4wide",
    "sines_x",
    "sines_yz",
    "gains",
    "packed1",
    "packed2",
    "packed3",
    "load_sem",
    "halo_send",
    "halo_recv",
    "part_send",
    "part_recv",
    "gy_send",
    "gy_recv",
    "gx_send",
    "gx_recv",
]


def sine_table(row, col, count):
    period = 2.0 * (count + 1)
    turns = (row + 1.0) * (col + 1.0)
    turns = turns - period * jnp.floor((turns + 0.5) * (1.0 / period))
    turns = turns - (count + 1.0)
    size = jnp.abs(turns)
    size = jnp.minimum(size, (count + 1.0) - size)
    angle = size * (math.pi / (count + 1))
    square = angle * angle
    total = 1.0
    for order in (12, 10, 8, 6, 4, 2):
        total = 1.0 - total * square * (1.0 / (order * (order + 1)))
    value = angle * total * math.sqrt(2.0 / (count + 1))
    return jnp.where(turns < 0.0, value, -value)


def coarse_tables(sines_x, sines_yz, gains):
    def places(shape):
        return [lax.broadcasted_iota(jnp.int32, shape, axis) for axis in range(2)]

    def real(numbers):
        return numbers.astype(jnp.float32)

    row, col = places((80, LANES))
    inside = (row >= 8) & (row < 72) & (col < 64)
    sines_x[...] = jnp.where(inside, sine_table(real(row - 8), real(col), 64), 0.0)
    for tile in range(8):
        row, col = places((32, 256))
        row = row + 32 * tile
        sines_yz[32 * tile : 32 * tile + 32, :] = sine_table(
            real(row >> 3), real(col >> 3), 32
        ) * sine_table(real(row & 7), real(col & 7), 8)

    def value(place, count):
        sine = sine_table(real(place), jnp.zeros(place.shape, jnp.float32), 2 * count + 1)
        return (4.0 * (count + 1)) * sine * sine

    row, col = places((64, 256))
    damped = (JACOBI_WEIGHT / 6.0) * (value(row, 64) + value(col >> 3, 32) + value(col & 7, 8))
    kept = 1.0 - damped
    power = kept * kept
    power = power * power
    fourth = power
    power = power * power
    power = power * power * fourth
    assert JACOBI == 20
    gains[...] = (JACOBI_WEIGHT * 4.0**LEVELS / 6.0) * (1.0 - power) / damped


def ring(step, count):
    return min(step % count, -step % count)


def hops_x(step):
    return sum(ring((core + step) // 2 - core // 2, 8) for core in range(2))


def hops_y(step):
    return sum(ring((x + step) // 4, 4) + ring((x + step) % 4 - x, 4) for x in range(4))


FAR_FIRST = {
    "gx": sorted(range(1, N), key=hops_x, reverse=True),
    "gy": sorted(range(1, N), key=hops_y, reverse=True),
}


def overlap(step, block, spread):
    low = max(-spread, step * block - HALO)
    high = min(block + spread, step * block + block + HALO)
    return low, high - low, low - step * block


def groups(step, level):
    low, many, _ = overlap(step, BX[level], SPREAD[level])
    low += SPREAD[level]
    first = low // GROUP[level]
    last = -(-(low + many) // GROUP[level])
    return first, last - first, low - first * GROUP[level]


def lanes_of(shape):
    return lax.broadcasted_iota(jnp.int32, shape, len(shape) - 1)


def along_z(cells, level):
    step = 1 << level
    axis = cells.ndim - 1
    lane = lanes_of(cells.shape)
    below = jnp.where(lane >= step, pltpu.roll(cells, step, axis), 0.0)
    above = jnp.where(lane < LANES - step, pltpu.roll(cells, LANES - step, axis), 0.0)
    return below + above


def pair_z(cells, level):
    step = 1 << level
    axis = cells.ndim - 1
    odd = (lanes_of(cells.shape) >> level) & 1
    other = jnp.where(odd == 0, pltpu.roll(cells, LANES - step, axis), pltpu.roll(cells, step, axis))
    return cells + other


def pack(rows, size):
    count, wide = rows.shape[0] // size, rows.shape[1]
    rows = rows.reshape(count, size, wide, LANES)
    which = lanes_of((count, wide, LANES)) & (size - 1)
    packed = rows[:, size - 1]
    for index in range(size - 1):
        packed = jnp.where(which == index, rows[:, index], packed)
    return packed


def unpack(packed, size):
    lane = lanes_of(packed.shape)
    rows = [packed]
    bit = 1
    while bit < size:
        even = [jnp.where((lane & bit) == 0, row, pltpu.roll(row, bit, 2)) for row in rows]
        odd = [jnp.where((lane & bit) == 0, pltpu.roll(row, LANES - bit, 2), row) for row in rows]
        rows = even + odd
        bit *= 2
    return jnp.stack(rows, axis=1).reshape(size * packed.shape[0], packed.shape[1], LANES)


def around(ref, row, count, level, start, wide):
    tall = ref[pl.ds(row - 1, count + 2), start : start + wide, :]
    center = tall[1 : count + 1]
    total = tall[:count] + tall[2:]
    total = total + ref[pl.ds(row, count), start - 1 : start - 1 + wide, :]
    total = total + ref[pl.ds(row, count), start + 1 : start + 1 + wide, :]
    return center, total + along_z(center, level)


def inside_y(level, start, wide, scale=1.0):
    place = lax.broadcasted_iota(jnp.int32, (wide, LANES), 0) + (start - OY)
    place = place + lax.axis_index("gy") * BY[level]
    return jnp.where((place >= 0) & (place < N * BY[level]), scale, 0.0)


def clip_x(ref, level, halo, start, wide):
    gx = lax.axis_index("gx")
    first = OX[level]
    last = first + BX[level]
    ref[first - halo : first, start : start + wide, :] *= jnp.where(gx > 0, 1.0, 0.0)
    ref[last : last + halo, start : start + wide, :] *= jnp.where(gx < N - 1, 1.0, 0.0)


def chunks(first, count, size, body):
    assert count % size == 0
    for index in range(count // size):
        body(first + index * size)


def kernel(density, e1_out, relaxed_low, relaxed_high, source_low, source_high, *scratch):
    names = [kind + str(level) for kind in KINDS for level in range(LEVELS)] + SINGLE
    refs = dict(zip(names, scratch))
    inbox = dict(zip([(k, d) for k in range(LEVELS) for d in PARTNERS[k]], scratch[len(names) :]))
    own = [refs[f"own{k}"] for k in range(4)]
    ownx = [refs[f"ownx{k}"] for k in range(4)]
    b = [own[0]] + [refs[f"b{k}"] for k in (1, 2, 3)]
    x = [refs[f"x{k}"] for k in range(4)]
    f = [refs[f"f{k}"] for k in range(4)]
    e = [None, e1_out, refs["e2"], refs["e3"]]
    pairs, packer, spreader = refs["pairs"], refs["packer"], refs["spreader"]

    gx, gy = lax.axis_index("gx"), lax.axis_index("gy")

    def device(step):
        return {"gx": lax.rem(gx + step[0] + N, N), "gy": lax.rem(gy + step[1] + N, N)}

    barrier = pltpu.get_barrier_semaphore()
    for step in EVERYONE:
        pl.semaphore_signal(barrier, inc=1, device_id=device(step), device_id_type=MESH)

    loads = [
        pltpu.make_async_copy(
            density.at[16 * part : 16 * part + 16],
            own[0].at[4 + 16 * part : 20 + 16 * part, 8:40, :],
            refs["load_sem"].at[part],
        )
        for part in range(4)
    ]
    for copy in loads:
        copy.start()

    def zero(ref, rows, cols):
        ref[rows[0] : rows[1], cols[0] : cols[1], :] = jnp.zeros(
            (rows[1] - rows[0], cols[1] - cols[0], LANES), jnp.float32
        )

    for ref in (own[0], ownx[0]):
        zero(ref, (0, 4), (0, 48))
        zero(ref, (68, 72), (0, 48))
        zero(ref, (4, 68), (0, 8))
        zero(ref, (4, 68), (40, 48))
    zero(refs["f0"], (0, 2), (0, 48))
    zero(refs["f0"], (70, 72), (0, 48))
    for level in (1, 2, 3):
        zero(own[level], (0, ROWS[level]), (0, COLS[level]))
        zero(ownx[level], (0, ROWS[level]), (0, COLS[level]))
        zero(b[level], (0, ROWS[level]), (0, COLS[level]))
    row = lax.broadcasted_iota(jnp.int32, (768, LANES), 0)
    col = lax.broadcasted_iota(jnp.int32, (768, LANES), 1)
    hit = ((row & 7) == 0) & (((row >> 4) & 7) == (col & 7)) & ((row >> 7) == (col >> 3))
    packer[...] = jnp.where(hit, 0.125, 0.0)
    row = lax.broadcasted_iota(jnp.int32, (LANES, 768), 0)
    col = lax.broadcasted_iota(jnp.int32, (LANES, 768), 1)
    hit = ((row >> 3) == (col >> 7)) & ((row & 7) == ((col >> 4) & 7))
    spreader[...] = jnp.where(hit, 1.0, 0.0)

    def presmooth(source, out, level, halo, size, ready=None):
        inverse = 0.25**level
        scale_first = WEIGHT_FIRST * 4.0**level / 6.0
        scale_second = WEIGHT_SECOND * 4.0**level / 6.0
        linear = scale_first + scale_second
        mixed = scale_first * scale_second * inverse
        start, wide = START, WIDE[level]
        inside = inside_y(level, start, wide)

        def body(row):
            if ready is not None:
                ready(row + size)
            center, total = around(source, row, size, level, start, wide)
            out[pl.ds(row, size), start : start + wide, :] = (
                (linear - 6.0 * mixed) * center + mixed * total
            ) * inside

        chunks(OX[level] - halo, BX[level] + 2 * halo, size, body)
        clip_x(out, level, halo, start, wide)

    def down(source, field, out, level, first, count, size):
        inverse = 0.25**level
        start, wide = START, WIDE[level]
        half = wide // 2

        def body(coarse):
            row = OX[level] + 2 * coarse
            center, total = around(field, row, 2 * size, level, start, wide)
            rest = source[pl.ds(row, 2 * size), start : start + wide, :] - inverse * (6.0 * center - total)
            rest = rest.reshape(size, 2, wide, LANES)
            at = pl.ds(coarse - first, size)
            pairs[at, :wide, :] = rest[:, 0] + rest[:, 1]
            both = pairs[at, pl.ds(0, half, stride=2), :] + pairs[at, pl.ds(1, half, stride=2), :]
            out(coarse, both, size)

        chunks(first, count, size, body)

    def store_level(level):
        start, wide = OY - 2, WIDE[level - 1] // 2
        inside = inside_y(level, start, wide)

        def out(coarse, both, size):
            own[level][pl.ds(OX[level] + coarse, size), start : start + wide, :] = (
                0.125 * pair_z(both, level - 1) * inside
            )
        return out

    waiting = list(loads)

    def loaded(row):
        while waiting and (row >= 4 + 16 * (4 - len(waiting)) or row >= 67):
            waiting.pop(0).wait()

    presmooth(own[0], ownx[0], 0, 1, 11, loaded)

    down(own[0], ownx[0], store_level(1), 0, -1, 34, 2)
    clip_x(own[1], 1, SPREAD[1], OY - 2, WIDE[0] // 2)
    presmooth(own[1], ownx[1], 1, 2, 4)
    down(own[1], ownx[1], store_level(2), 1, -2, 20, 2)
    clip_x(own[2], 2, SPREAD[2], OY - 2, WIDE[1] // 2)
    presmooth(own[2], ownx[2], 2, 3, 11)
    down(own[2], ownx[2], store_level(3), 2, -2, 12, 4)
    clip_x(own[3], 3, SPREAD[3], OY - 2, WIDE[2] // 2)
    presmooth(own[3], ownx[3], 3, 3, 14)

    def store_cells(coarse, both, size):
        for index in range(size):
            refs["cells4"][8 * index : 8 * index + 8, :] = both[index]

    down(own[3], ownx[3], store_cells, 3, -2, 8, 8)
    part = jnp.zeros((8, LANES), jnp.float32)
    for place in range(6):
        part = part + jnp.dot(
            refs["cells4"][pl.ds(place, 8, stride=8), :],
            packer[place * LANES : (place + 1) * LANES, :],
            precision=lax.Precision.HIGHEST,
            preferred_element_type=jnp.float32,
        )
    place_x = lax.broadcasted_iota(jnp.int32, (8, LANES), 0) - 2 + gx * BX[4]
    place_y = (lanes_of((8, LANES)) >> 3) - 2 + gy * BY[4]
    inside = (place_x >= 0) & (place_x < N * BX[4]) & (place_y >= 0) & (place_y < N * BY[4])
    part = jnp.where(inside, part, 0.0)
    refs["part4"][...] = part

    def line_copy(axis, step, slot):
        source, slots = (refs["part4"], refs["gathery"]) if axis == "gy" else (refs["strip"], refs["gatherx"])
        return pltpu.make_async_remote_copy(
            src_ref=source,
            dst_ref=slots.at[slot],
            send_sem=refs[axis + "_send"].at[step],
            recv_sem=refs[axis + "_recv"].at[slot],
            device_id=device((step, 0) if axis == "gx" else (0, step)),
            device_id_type=MESH,
        )

    pl.semaphore_wait(barrier, len(EVERYONE))
    sent = []
    for step in FAR_FIRST["gy"]:
        copy = line_copy("gy", step, gy)
        copy.start()
        sent.append(copy)

    parts = {}
    for level in (3, 2, 1):
        spread = SPREAD[level]
        first = OX[level] - spread
        wide = BY[level] + 2 * spread
        packed = refs["packed" + str(level)]
        packed[:, OY : OY + wide, :] = pack(
            own[level][first : first + BX[level] + 2 * spread, OY - spread : OY - spread + wide, :],
            GROUP[level],
        )
        for step in PARTNERS[level]:
            index = len(parts)
            first, count, _ = groups(step[0], level)
            low_y, many_y, _ = overlap(step[1], BY[level], spread)
            low_y += OY + spread
            copy = pltpu.make_async_remote_copy(
                src_ref=packed.at[first : first + count, low_y : low_y + many_y, :],
                dst_ref=inbox[level, step],
                send_sem=refs["part_send"].at[index],
                recv_sem=refs["part_recv"].at[index],
                device_id=device(step),
                device_id_type=MESH,
            )
            copy.start()
            parts[level, step] = copy
            sent.append(copy)

    def relax(field, out, level, weight, halo, size, scale=1.0):
        scale_now = weight * 4.0**level / 6.0
        start, wide = START, WIDE[level]
        inside = inside_y(level, start, wide, scale)

        def body(row):
            center, total = around(field, row, size, level, start, wide)
            source = b[level][pl.ds(row, size), start : start + wide, :]
            result = ((1.0 - weight) * center + scale_now * source + (weight / 6.0) * total) * inside
            out[pl.ds(row, size), start : start + wide, :] = result

        chunks(OX[level] - halo, BX[level] + 2 * halo, size, body)
        clip_x(out, level, halo, start, wide)

    coarse_tables(refs["sines_x"], refs["sines_yz"], refs["gains"])
    relax(ownx[0], f[0], 0, WEIGHT_FIRST, 2, 17)
    relax(f[0], x[0], 0, WEIGHT_SECOND, SPREAD0, 14, FOUR_PI)

    def side(step, block):
        low = max(-SPREAD0, step * block - 1)
        high = min(block + SPREAD0, step * block + block + 1)
        return low, high - low, low - step * block + 1

    strips = []
    for index, step in enumerate(AROUND):
        low_x, many_x, _ = side(step[0], BX[0])
        low_y, many_y, _ = side(step[1], BY[0])
        copy = pltpu.make_async_remote_copy(
            src_ref=x[0].at[OX[0] + low_x : OX[0] + low_x + many_x, OY + low_y : OY + low_y + many_y, :],
            dst_ref=inbox[0, step],
            send_sem=refs["halo_send"].at[index],
            recv_sem=refs["halo_recv"].at[index],
            device_id=device(step),
            device_id_type=MESH,
        )
        copy.start()
        strips.append(copy)
        sent.append(copy)
    for step in range(1, N):
        slot = lax.rem(gy + N - step, N)
        line_copy("gy", step, slot).wait_recv()
    refs["gathery"][gy] = refs["part4"][...]
    lane = lanes_of((8, LANES))
    near = jnp.zeros((8, LANES), jnp.float32)
    far = jnp.zeros((8, LANES), jnp.float32)
    for slot in range(N):
        moved = pltpu.roll(refs["gathery"][slot], (16 * slot - 16) % LANES, 1)
        if slot < 7:
            near = near + moved
        elif slot > 8:
            far = far + moved
        else:
            low = jnp.where(lane >= 64, moved, 0.0)
            near = near + low
            far = far + (moved - low)
    refs["strip"][0:8, :] = near
    refs["strip"][8:16, :] = far
    for step in FAR_FIRST["gx"]:
        copy = line_copy("gx", step, gx)
        copy.start()
        sent.append(copy)

    for level in (3, 2, 1):
        spread = SPREAD[level]
        first_x, first_y = OX[level], OY
        rows = slice(first_x - spread, first_x + BX[level] + spread)
        cols = slice(first_y - spread, first_y + BY[level] + spread)
        b[level][rows, cols, :] = own[level][rows, cols, :]
        for step in PARTNERS[level]:
            parts[level, step].wait_recv()
            _, many_x, to_x = overlap(step[0], BX[level], spread)
            _, many_y, to_y = overlap(step[1], BY[level], spread)
            skip = groups(step[0], level)[2]
            rows = unpack(inbox[level, step][...], GROUP[level])
            b[level][
                first_x + to_x : first_x + to_x + many_x, first_y + to_y : first_y + to_y + many_y, :
            ] += rows[skip : skip + many_x]
        cover = BY[level] + 2 * HALO
        inside = inside_y(level, OY - HALO, cover)
        b[level][:, OY - HALO : OY - HALO + cover, :] *= inside
        clip_x(b[level], level, HALO, OY - HALO, cover)
        presmooth(b[level], x[level], level, 4, {3: 8, 2: 8, 1: 4}[level])

    source_low[...] = FOUR_PI * own[0][4:36, 8:40, :]
    source_high[...] = FOUR_PI * own[0][36:68, 8:40, :]
    relaxed_low[...] = x[0][3:36, START : START + WIDE[0], :]
    relaxed_high[...] = x[0][36:69, START : START + WIDE[0], :]
    for index, step in enumerate(AROUND):
        strips[index].wait_recv()
        _, many_x, to_x = side(step[0], BX[0])
        _, many_y, to_y = side(step[1], BY[0])
        to_y += OY - 1 - START
        for half, target in enumerate((relaxed_low, relaxed_high)):
            low, high = max(to_x, 33 * half), min(to_x + many_x, 33 * half + 33)
            if low < high:
                target[low - 33 * half : high - 33 * half, to_y : to_y + many_y, :] += inbox[0, step][
                    low - to_x : high - to_x
                ]

    for step in range(1, N):
        slot = lax.rem(gx + N - step, N)
        line_copy("gx", step, slot).wait_recv()
    refs["gatherx"][gx] = refs["strip"][...]
    b4 = refs["b4"]
    b4[...] = jnp.zeros((80, 256), jnp.float32)
    for slot in range(N):
        for tile in range(2):
            at = (slice(6 + 4 * slot, 14 + 4 * slot), slice(LANES * tile, LANES * tile + LANES))
            b4[at] += refs["gatherx"][slot, 8 * tile : 8 * tile + 8, :]

    def times(one, other):
        return jnp.dot(
            one, other, precision=lax.Precision.HIGHEST, preferred_element_type=jnp.float32
        )

    sines_yz = refs["sines_yz"][...]
    waves = times(refs["sines_x"][8:72, :64], b4[8:72, :])
    waves = times(waves, sines_yz) * refs["gains"][...]
    waves = times(refs["sines_x"][pl.ds(6 + 4 * gx, 8), :64], waves)
    coarsest = times(waves, sines_yz)

    lane = lanes_of((8, LANES))
    back = lax.rem(16 - 16 * gy + 2 * LANES, LANES)
    place = lane + 16 * gy - 16
    near = pltpu.roll(coarsest[:, :LANES], back, 1)
    far = pltpu.roll(coarsest[:, LANES:], back, 1)
    mine = jnp.where((place >= 0) & (place < LANES), near, 0.0)
    mine = jnp.where((place >= LANES) & (place < 2 * LANES), far, mine)
    wide4 = times(mine, spreader[...])
    for place in range(6):
        refs["e4wide"][pl.ds(place, 8, stride=8), :] = wide4[:, place * LANES : (place + 1) * LANES]

    def correct(level, first, count, size):
        half = 6 if level == 3 else WIDE[level] // 2

        def body(coarse):
            if level == 3:
                fix = refs["e4wide"][...].reshape(8, 8, LANES)[:, :half]
            else:
                fix = e[level + 1][pl.ds(OX[level + 1] + coarse, size), OY - 2 : OY - 2 + half, :]
            fix = jnp.broadcast_to(fix[:, None], (size, 2, half, LANES)).reshape(2 * size, half, LANES)
            row = OX[level] + 2 * coarse
            for parity in range(2):
                place = (pl.ds(row, 2 * size), pl.ds(START + parity, half, stride=2), slice(None))
                x[level][place] = x[level][place] + fix
        chunks(first, count, size, body)

    correct(3, -2, 8, 8)
    relax(x[3], f[3], 3, WEIGHT_FIRST, 3, 14)
    relax(f[3], e[3], 3, WEIGHT_SECOND, 2, 12)
    correct(2, -2, 12, 6)
    relax(x[2], f[2], 2, WEIGHT_FIRST, 3, 11)
    relax(f[2], e[2], 2, WEIGHT_SECOND, 2, 10)
    correct(1, -2, 20, 4)
    relax(x[1], f[1], 1, WEIGHT_FIRST, 4, 4)
    relax(f[1], e[1], 1, WEIGHT_SECOND, 2, 4)

    for copy in sent:
        copy.wait_send()


def finish(
    e1, relaxed_low, relaxed_high, source_low, source_high, potential, residual, first, pot, out, out_sem
):
    relaxed = (relaxed_low, relaxed_high)
    source = (source_low, source_high)

    inside = inside_y(1, OY - 1, 18, FOUR_PI)

    def spread(coarse):
        rows = pl.ds(OX[1] + coarse, 17)
        cells = e1[rows, OY - 1 : OY + 17, :]
        same = (1.0 - WEIGHT_FIRST * 2.0 / 3.0) * cells + (WEIGHT_FIRST / 6.0) * along_z(cells, 0)
        same = same * inside
        share = inside * (WEIGHT_FIRST / 6.0)
        for odd_x in range(2):
            beside = e1[pl.ds(OX[1] + coarse + 2 * odd_x - 1, 17), OY - 1 : OY + 17, :]
            for odd_y in range(2):
                below = OY - 2 + 2 * odd_y
                both = beside + e1[rows, below : below + 18, :]
                both = same + share * both
                for index in range(17):
                    row = OX[0] + 2 * (coarse + index) + odd_x
                    first[row, pl.ds(OY - 2 + odd_y, 18, stride=2), :] = both[index]

    chunks(-1, 34, 17, spread)
    clip_x(first, 0, 2, START, WIDE[0])

    inside = inside_y(0, START, WIDE[0])
    cols = slice(START, START + WIDE[0])

    def second(row):
        center, total = around(first, row, 11, 0, START, WIDE[0])
        later = (1.0 - WEIGHT_SECOND) * center + (WEIGHT_SECOND / 6.0) * total
        place = row - OX[0] + 1
        pot[pl.ds(row, 11), cols, :] = (
            relaxed[place // 33][pl.ds(place % 33, 11)] + later
        ) * inside

    def rest(row, count):
        center, total = around(pot, row, count, 0, OY, BY[0])
        place = row - OX[0]
        for half in range(2):
            low, high = max(place, 32 * half), min(place + count, 32 * half + 32)
            if low < high:
                part = slice(low - place, high - place)
                here = source[half][low - 32 * half : high - 32 * half]
                out[low:high] = here - 6.0 * center[part] + total[part]

    stores = []

    def store(origin, target, index, low, high):
        copy = pltpu.make_async_copy(
            origin, target.at[low:high], out_sem.at[index, len(stores) // 2]
        )
        copy.start()
        stores.append(copy)

    done_pot, done_rest = 0, 0
    for part in range(6):
        second(OX[0] - 1 + 11 * part)
        if part == 0:
            pot[3:4, cols, :] *= jnp.where(lax.axis_index("gx") > 0, 1.0, 0.0)
        if part == 5:
            pot[68:69, cols, :] *= jnp.where(lax.axis_index("gx") < N - 1, 1.0, 0.0)
        ready = 11 * part + 10
        low, done_pot = done_pot, min(ready, BX[0])
        store(pot.at[4 + low : 4 + done_pot, OY : OY + BY[0], :], potential, 0, low, done_pot)
        low, done_rest = done_rest, min(ready - 1, BX[0])
        rest(OX[0] + low, done_rest - low)
        store(out.at[low:done_rest], residual, 1, low, done_rest)
    for copy in stores:
        copy.wait()


def on_device(density):
    def cells(*shape):
        return pltpu.VMEM(shape + (LANES,), jnp.float32)

    level_arrays = [cells(ROWS[k], COLS[k]) for k in range(4)]
    dma = pltpu.SemaphoreType.DMA
    scratch = level_arrays * 6 + [
        cells(34, 40),
        cells(768),
        pltpu.VMEM((LANES, 768), jnp.float32),
        cells(64),
        cells(8),
        cells(N, 8),
        cells(16),
        cells(N, 16),
        pltpu.VMEM((80, 256), jnp.float32),
        cells(64),
        cells(80),
        pltpu.VMEM((256, 256), jnp.float32),
        pltpu.VMEM((64, 256), jnp.float32),
        cells(17, 32),
        cells(5, 24),
        cells(3, 24),
        dma((4,)),
        dma((8,)),
        dma((8,)),
        dma((30,)),
        dma((30,)),
        dma((N,)),
        dma((N,)),
        dma((N,)),
        dma((N,)),
    ]
    for dx, dy in AROUND:
        scratch.append(cells(SPREAD0 + 1 if dx else BX[0] + 2, SPREAD0 + 1 if dy else BY[0] + 2))
    for level in (1, 2, 3):
        for step in PARTNERS[level]:
            many_y = overlap(step[1], BY[level], SPREAD[level])[1]
            scratch.append(cells(groups(step[0], level)[1], many_y))
    hbm = pl.BlockSpec(memory_space=pltpu.HBM)
    vmem = pl.BlockSpec(memory_space=pltpu.VMEM)
    shapes = [(ROWS[1], COLS[1])] + [(33, WIDE[0])] * 2 + [(32, 32)] * 2
    shared = pl.pallas_call(
        kernel,
        out_shape=[jax.ShapeDtypeStruct(shape + (LANES,), jnp.float32) for shape in shapes],
        in_specs=[hbm],
        out_specs=[vmem] * 5,
        scratch_shapes=scratch,
        compiler_params=pltpu.CompilerParams(
            collective_id=0, has_side_effects=True, vmem_limit_bytes=50 * 2**20 + 2**18
        ),
        name="vcycle",
    )(density)
    return pl.pallas_call(
        finish,
        out_shape=[jax.ShapeDtypeStruct(density.shape, jnp.float32)] * 2,
        in_specs=[vmem] * 5,
        out_specs=[hbm] * 2,
        scratch_shapes=[
            cells(ROWS[0], COLS[0]),
            cells(ROWS[0], COLS[0]),
            cells(64, 32),
            dma((2, 6)),
        ],
        compiler_params=pltpu.CompilerParams(vmem_limit_bytes=24 * 2**20),
        name="finish",
    )(*shared)


def solution(mesh):
    return jax.shard_map(
        on_device,
        mesh=mesh,
        in_specs=(P("gx", "gy", None),),
        out_specs=(P("gx", "gy", None), P("gx", "gy", None)),
        check_vma=False,
    )
```

```python
import math

import jax
import jax.numpy as jnp
from jax import lax
from jax.experimental import pallas as pl
from jax.experimental.pallas import tpu as pltpu
from jax.sharding import PartitionSpec as P

LEVELS = 4
JACOBI = 20
FOUR_PI = 4.0 * math.pi
WEIGHT_FIRST = 1.0 / (1.25 + 0.75 * math.cos(math.pi / 4.0))
WEIGHT_SECOND = 1.0 / (1.25 - 0.75 * math.cos(math.pi / 4.0))
JACOBI_WEIGHT = 0.8

N = 16
LANES = 128
BX = (64, 32, 16, 8, 4)
BY = (32, 16, 8, 4, 2)
OX = (4, 6, 6, 6)
OY = 8
ROWS = (72, 44, 28, 20)
COLS = (48, 32, 24, 24)
START = 4
WIDE = (40, 24, 16, 16)
SPREAD = (0, 1, 2, 2)
HALO = 5
GROUP = (1, 2, 4, 4)
SPREAD0 = 3
MESH = pl.DeviceIdType.MESH

AROUND = [(dx, dy) for dx in (-1, 0, 1) for dy in (-1, 0, 1) if (dx, dy) != (0, 0)]
AROUND3 = [(dx, dy) for dx in (-1, 0, 1) for dy in (-2, -1, 0, 1, 2) if (dx, dy) != (0, 0)]
PARTNERS = {0: AROUND, 1: AROUND, 2: AROUND, 3: AROUND3}
EVERYONE = sorted(
    {(dx % N, dy % N) for dx, dy in AROUND3}
    | {(d, 0) for d in range(1, N)}
    | {(0, d) for d in range(1, N)}
)

KINDS = ["own", "ownx", "b", "x", "f", "e"]
SINGLE = [
    "pairs",
    "packer",
    "spreader",
    "cells4",
    "part4",
    "gathery",
    "strip",
    "gatherx",
    "b4",
    "e4wide",
    "sines_x",
    "sines_yz",
    "gains",
    "packed1",
    "packed2",
    "packed3",
    "load_sem",
    "halo_send",
    "halo_recv",
    "part_send",
    "part_recv",
    "gy_send",
    "gy_recv",
    "gx_send",
    "gx_recv",
]


def sine_table(row, col, count):
    period = 2.0 * (count + 1)
    turns = (row + 1.0) * (col + 1.0)
    turns = turns - period * jnp.floor((turns + 0.5) * (1.0 / period))
    turns = turns - (count + 1.0)
    size = jnp.abs(turns)
    size = jnp.minimum(size, (count + 1.0) - size)
    angle = size * (math.pi / (count + 1))
    square = angle * angle
    total = 1.0
    for order in (12, 10, 8, 6, 4, 2):
        total = 1.0 - total * square * (1.0 / (order * (order + 1)))
    value = angle * total * math.sqrt(2.0 / (count + 1))
    return jnp.where(turns < 0.0, value, -value)


def coarse_tables(sines_x, sines_yz, gains):
    def places(shape):
        return [lax.broadcasted_iota(jnp.int32, shape, axis) for axis in range(2)]

    def real(numbers):
        return numbers.astype(jnp.float32)

    row, col = places((80, LANES))
    inside = (row >= 8) & (row < 72) & (col < 64)
    sines_x[...] = jnp.where(inside, sine_table(real(row - 8), real(col), 64), 0.0)
    for tile in range(8):
        row, col = places((32, 256))
        row = row + 32 * tile
        sines_yz[32 * tile : 32 * tile + 32, :] = sine_table(
            real(row >> 3), real(col >> 3), 32
        ) * sine_table(real(row & 7), real(col & 7), 8)

    def value(place, count):
        sine = sine_table(real(place), jnp.zeros(place.shape, jnp.float32), 2 * count + 1)
        return (4.0 * (count + 1)) * sine * sine

    row, col = places((64, 256))
    damped = (JACOBI_WEIGHT / 6.0) * (value(row, 64) + value(col >> 3, 32) + value(col & 7, 8))
    kept = 1.0 - damped
    power = kept * kept
    power = power * power
    fourth = power
    power = power * power
    power = power * power * fourth
    assert JACOBI == 20
    gains[...] = (JACOBI_WEIGHT * 4.0**LEVELS / 6.0) * (1.0 - power) / damped


def ring(step, count):
    return min(step % count, -step % count)


def hops_x(step):
    return sum(ring((core + step) // 2 - core // 2, 8) for core in range(2))


def hops_y(step):
    return sum(ring((x + step) // 4, 4) + ring((x + step) % 4 - x, 4) for x in range(4))


FAR_FIRST = {
    "gx": sorted(range(1, N), key=hops_x, reverse=True),
    "gy": sorted(range(1, N), key=hops_y, reverse=True),
}


def overlap(step, block, spread):
    low = max(-spread, step * block - HALO)
    high = min(block + spread, step * block + block + HALO)
    return low, high - low, low - step * block


def groups(step, level):
    low, many, _ = overlap(step, BX[level], SPREAD[level])
    low += SPREAD[level]
    first = low // GROUP[level]
    last = -(-(low + many) // GROUP[level])
    return first, last - first, low - first * GROUP[level]


def lanes_of(shape):
    return lax.broadcasted_iota(jnp.int32, shape, len(shape) - 1)


def along_z(cells, level):
    step = 1 << level
    axis = cells.ndim - 1
    lane = lanes_of(cells.shape)
    below = jnp.where(lane >= step, pltpu.roll(cells, step, axis), 0.0)
    above = jnp.where(lane < LANES - step, pltpu.roll(cells, LANES - step, axis), 0.0)
    return below + above


def pair_z(cells, level):
    step = 1 << level
    axis = cells.ndim - 1
    odd = (lanes_of(cells.shape) >> level) & 1
    other = jnp.where(odd == 0, pltpu.roll(cells, LANES - step, axis), pltpu.roll(cells, step, axis))
    return cells + other


def pack(rows, size):
    count, wide = rows.shape[0] // size, rows.shape[1]
    rows = rows.reshape(count, size, wide, LANES)
    which = lanes_of((count, wide, LANES)) & (size - 1)
    packed = rows[:, size - 1]
    for index in range(size - 1):
        packed = jnp.where(which == index, rows[:, index], packed)
    return packed


def unpack(packed, size):
    lane = lanes_of(packed.shape)
    rows = [packed]
    bit = 1
    while bit < size:
        even = [jnp.where((lane & bit) == 0, row, pltpu.roll(row, bit, 2)) for row in rows]
        odd = [jnp.where((lane & bit) == 0, pltpu.roll(row, LANES - bit, 2), row) for row in rows]
        rows = even + odd
        bit *= 2
    return jnp.stack(rows, axis=1).reshape(size * packed.shape[0], packed.shape[1], LANES)


def around(ref, row, count, level, start, wide):
    tall = ref[pl.ds(row - 1, count + 2), start : start + wide, :]
    center = tall[1 : count + 1]
    total = tall[:count] + tall[2:]
    total = total + ref[pl.ds(row, count), start - 1 : start - 1 + wide, :]
    total = total + ref[pl.ds(row, count), start + 1 : start + 1 + wide, :]
    return center, total + along_z(center, level)


def inside_y(level, start, wide, scale=1.0):
    place = lax.broadcasted_iota(jnp.int32, (wide, LANES), 0) + (start - OY)
    place = place + lax.axis_index("gy") * BY[level]
    return jnp.where((place >= 0) & (place < N * BY[level]), scale, 0.0)


def clip_x(ref, level, halo, start, wide):
    gx = lax.axis_index("gx")
    first = OX[level]
    last = first + BX[level]
    ref[first - halo : first, start : start + wide, :] *= jnp.where(gx > 0, 1.0, 0.0)
    ref[last : last + halo, start : start + wide, :] *= jnp.where(gx < N - 1, 1.0, 0.0)


def chunks(first, count, size, body):
    assert count % size == 0
    for index in range(count // size):
        body(first + index * size)


def kernel(density, e1_out, relaxed_low, relaxed_high, source_low, source_high, *scratch):
    names = [kind + str(level) for kind in KINDS for level in range(LEVELS)] + SINGLE
    refs = dict(zip(names, scratch))
    inbox = dict(zip([(k, d) for k in range(LEVELS) for d in PARTNERS[k]], scratch[len(names) :]))
    own = [refs[f"own{k}"] for k in range(4)]
    ownx = [refs[f"ownx{k}"] for k in range(4)]
    b = [own[0]] + [refs[f"b{k}"] for k in (1, 2, 3)]
    x = [refs[f"x{k}"] for k in range(4)]
    f = [refs[f"f{k}"] for k in range(4)]
    e = [None, e1_out, refs["e2"], refs["e3"]]
    pairs, packer, spreader = refs["pairs"], refs["packer"], refs["spreader"]

    gx, gy = lax.axis_index("gx"), lax.axis_index("gy")

    def device(step):
        return {"gx": lax.rem(gx + step[0] + N, N), "gy": lax.rem(gy + step[1] + N, N)}

    barrier = pltpu.get_barrier_semaphore()
    for step in EVERYONE:
        pl.semaphore_signal(barrier, inc=1, device_id=device(step), device_id_type=MESH)

    loads = [
        pltpu.make_async_copy(
            density.at[16 * part : 16 * part + 16],
            own[0].at[4 + 16 * part : 20 + 16 * part, 8:40, :],
            refs["load_sem"].at[part],
        )
        for part in range(4)
    ]
    for copy in loads:
        copy.start()

    def zero(ref, rows, cols):
        ref[rows[0] : rows[1], cols[0] : cols[1], :] = jnp.zeros(
            (rows[1] - rows[0], cols[1] - cols[0], LANES), jnp.float32
        )

    for ref in (own[0], ownx[0]):
        zero(ref, (0, 4), (0, 48))
        zero(ref, (68, 72), (0, 48))
        zero(ref, (4, 68), (0, 8))
        zero(ref, (4, 68), (40, 48))
    zero(refs["f0"], (0, 2), (0, 48))
    zero(refs["f0"], (70, 72), (0, 48))
    for level in (1, 2, 3):
        zero(own[level], (0, ROWS[level]), (0, COLS[level]))
        zero(ownx[level], (0, ROWS[level]), (0, COLS[level]))
        zero(b[level], (0, ROWS[level]), (0, COLS[level]))
    row = lax.broadcasted_iota(jnp.int32, (768, LANES), 0)
    col = lax.broadcasted_iota(jnp.int32, (768, LANES), 1)
    hit = ((row & 7) == 0) & (((row >> 4) & 7) == (col & 7)) & ((row >> 7) == (col >> 3))
    packer[...] = jnp.where(hit, 0.125, 0.0)
    row = lax.broadcasted_iota(jnp.int32, (LANES, 768), 0)
    col = lax.broadcasted_iota(jnp.int32, (LANES, 768), 1)
    hit = ((row >> 3) == (col >> 7)) & ((row & 7) == ((col >> 4) & 7))
    spreader[...] = jnp.where(hit, 1.0, 0.0)

    def presmooth(source, out, level, halo, size, ready=None):
        inverse = 0.25**level
        scale_first = WEIGHT_FIRST * 4.0**level / 6.0
        scale_second = WEIGHT_SECOND * 4.0**level / 6.0
        linear = scale_first + scale_second
        mixed = scale_first * scale_second * inverse
        start, wide = START, WIDE[level]
        inside = inside_y(level, start, wide)

        def body(row):
            if ready is not None:
                ready(row + size)
            center, total = around(source, row, size, level, start, wide)
            out[pl.ds(row, size), start : start + wide, :] = (
                (linear - 6.0 * mixed) * center + mixed * total
            ) * inside

        chunks(OX[level] - halo, BX[level] + 2 * halo, size, body)
        clip_x(out, level, halo, start, wide)

    def down(source, field, out, level, first, count, size):
        inverse = 0.25**level
        start, wide = START, WIDE[level]
        half = wide // 2

        def body(coarse):
            row = OX[level] + 2 * coarse
            center, total = around(field, row, 2 * size, level, start, wide)
            rest = source[pl.ds(row, 2 * size), start : start + wide, :] - inverse * (6.0 * center - total)
            rest = rest.reshape(size, 2, wide, LANES)
            at = pl.ds(coarse - first, size)
            pairs[at, :wide, :] = rest[:, 0] + rest[:, 1]
            both = pairs[at, pl.ds(0, half, stride=2), :] + pairs[at, pl.ds(1, half, stride=2), :]
            out(coarse, both, size)

        chunks(first, count, size, body)

    def store_level(level):
        start, wide = OY - 2, WIDE[level - 1] // 2
        inside = inside_y(level, start, wide)

        def out(coarse, both, size):
            own[level][pl.ds(OX[level] + coarse, size), start : start + wide, :] = (
                0.125 * pair_z(both, level - 1) * inside
            )
        return out

    waiting = list(loads)

    def loaded(row):
        while waiting and (row >= 4 + 16 * (4 - len(waiting)) or row >= 67):
            waiting.pop(0).wait()

    presmooth(own[0], ownx[0], 0, 1, 11, loaded)

    down(own[0], ownx[0], store_level(1), 0, -1, 34, 2)
    clip_x(own[1], 1, SPREAD[1], OY - 2, WIDE[0] // 2)
    presmooth(own[1], ownx[1], 1, 2, 4)
    down(own[1], ownx[1], store_level(2), 1, -2, 20, 2)
    clip_x(own[2], 2, SPREAD[2], OY - 2, WIDE[1] // 2)
    presmooth(own[2], ownx[2], 2, 3, 11)
    down(own[2], ownx[2], store_level(3), 2, -2, 12, 4)
    clip_x(own[3], 3, SPREAD[3], OY - 2, WIDE[2] // 2)
    presmooth(own[3], ownx[3], 3, 3, 14)

    def store_cells(coarse, both, size):
        for index in range(size):
            refs["cells4"][8 * index : 8 * index + 8, :] = both[index]

    down(own[3], ownx[3], store_cells, 3, -2, 8, 8)
    part = jnp.zeros((8, LANES), jnp.float32)
    for place in range(6):
        part = part + jnp.dot(
            refs["cells4"][pl.ds(place, 8, stride=8), :],
            packer[place * LANES : (place + 1) * LANES, :],
            precision=lax.Precision.HIGHEST,
            preferred_element_type=jnp.float32,
        )
    place_x = lax.broadcasted_iota(jnp.int32, (8, LANES), 0) - 2 + gx * BX[4]
    place_y = (lanes_of((8, LANES)) >> 3) - 2 + gy * BY[4]
    inside = (place_x >= 0) & (place_x < N * BX[4]) & (place_y >= 0) & (place_y < N * BY[4])
    part = jnp.where(inside, part, 0.0)
    refs["part4"][...] = part

    def line_copy(axis, step, slot):
        source, slots = (refs["part4"], refs["gathery"]) if axis == "gy" else (refs["strip"], refs["gatherx"])
        return pltpu.make_async_remote_copy(
            src_ref=source,
            dst_ref=slots.at[slot],
            send_sem=refs[axis + "_send"].at[step],
            recv_sem=refs[axis + "_recv"].at[slot],
            device_id=device((step, 0) if axis == "gx" else (0, step)),
            device_id_type=MESH,
        )

    pl.semaphore_wait(barrier, len(EVERYONE))
    sent = []
    for step in FAR_FIRST["gy"]:
        copy = line_copy("gy", step, gy)
        copy.start()
        sent.append(copy)

    parts = {}
    for level in (3, 2, 1):
        spread = SPREAD[level]
        first = OX[level] - spread
        wide = BY[level] + 2 * spread
        packed = refs["packed" + str(level)]
        packed[:, OY : OY + wide, :] = pack(
            own[level][first : first + BX[level] + 2 * spread, OY - spread : OY - spread + wide, :],
            GROUP[level],
        )
        for step in PARTNERS[level]:
            index = len(parts)
            first, count, _ = groups(step[0], level)
            low_y, many_y, _ = overlap(step[1], BY[level], spread)
            low_y += OY + spread
            copy = pltpu.make_async_remote_copy(
                src_ref=packed.at[first : first + count, low_y : low_y + many_y, :],
                dst_ref=inbox[level, step],
                send_sem=refs["part_send"].at[index],
                recv_sem=refs["part_recv"].at[index],
                device_id=device(step),
                device_id_type=MESH,
            )
            copy.start()
            parts[level, step] = copy
            sent.append(copy)

    def relax(field, out, level, weight, halo, size, scale=1.0):
        scale_now = weight * 4.0**level / 6.0
        start, wide = START, WIDE[level]
        inside = inside_y(level, start, wide, scale)

        def body(row):
            center, total = around(field, row, size, level, start, wide)
            source = b[level][pl.ds(row, size), start : start + wide, :]
            result = ((1.0 - weight) * center + scale_now * source + (weight / 6.0) * total) * inside
            out[pl.ds(row, size), start : start + wide, :] = result

        chunks(OX[level] - halo, BX[level] + 2 * halo, size, body)
        clip_x(out, level, halo, start, wide)

    coarse_tables(refs["sines_x"], refs["sines_yz"], refs["gains"])
    relax(ownx[0], f[0], 0, WEIGHT_FIRST, 2, 17)
    relax(f[0], x[0], 0, WEIGHT_SECOND, SPREAD0, 14, FOUR_PI)

    def side(step, block):
        low = max(-SPREAD0, step * block - 1)
        high = min(block + SPREAD0, step * block + block + 1)
        return low, high - low, low - step * block + 1

    strips = []
    for index, step in enumerate(AROUND):
        low_x, many_x, _ = side(step[0], BX[0])
        low_y, many_y, _ = side(step[1], BY[0])
        copy = pltpu.make_async_remote_copy(
            src_ref=x[0].at[OX[0] + low_x : OX[0] + low_x + many_x, OY + low_y : OY + low_y + many_y, :],
            dst_ref=inbox[0, step],
            send_sem=refs["halo_send"].at[index],
            recv_sem=refs["halo_recv"].at[index],
            device_id=device(step),
            device_id_type=MESH,
        )
        copy.start()
        strips.append(copy)
        sent.append(copy)
    for step in range(1, N):
        slot = lax.rem(gy + N - step, N)
        line_copy("gy", step, slot).wait_recv()
    refs["gathery"][gy] = refs["part4"][...]
    lane = lanes_of((8, LANES))
    near = jnp.zeros((8, LANES), jnp.float32)
    far = jnp.zeros((8, LANES), jnp.float32)
    for slot in range(N):
        moved = pltpu.roll(refs["gathery"][slot], (16 * slot - 16) % LANES, 1)
        if slot < 7:
            near = near + moved
        elif slot > 8:
            far = far + moved
        else:
            low = jnp.where(lane >= 64, moved, 0.0)
            near = near + low
            far = far + (moved - low)
    refs["strip"][0:8, :] = near
    refs["strip"][8:16, :] = far
    for step in FAR_FIRST["gx"]:
        copy = line_copy("gx", step, gx)
        copy.start()
        sent.append(copy)

    for level in (3, 2, 1):
        spread = SPREAD[level]
        first_x, first_y = OX[level], OY
        rows = slice(first_x - spread, first_x + BX[level] + spread)
        cols = slice(first_y - spread, first_y + BY[level] + spread)
        b[level][rows, cols, :] = own[level][rows, cols, :]
        for step in PARTNERS[level]:
            parts[level, step].wait_recv()
            _, many_x, to_x = overlap(step[0], BX[level], spread)
            _, many_y, to_y = overlap(step[1], BY[level], spread)
            skip = groups(step[0], level)[2]
            rows = unpack(inbox[level, step][...], GROUP[level])
            b[level][
                first_x + to_x : first_x + to_x + many_x, first_y + to_y : first_y + to_y + many_y, :
            ] += rows[skip : skip + many_x]
        cover = BY[level] + 2 * HALO
        inside = inside_y(level, OY - HALO, cover)
        b[level][:, OY - HALO : OY - HALO + cover, :] *= inside
        clip_x(b[level], level, HALO, OY - HALO, cover)
        presmooth(b[level], x[level], level, 4, {3: 8, 2: 8, 1: 4}[level])

    source_low[...] = FOUR_PI * own[0][4:36, 8:40, :]
    source_high[...] = FOUR_PI * own[0][36:68, 8:40, :]
    relaxed_low[...] = x[0][3:36, START : START + WIDE[0], :]
    relaxed_high[...] = x[0][36:69, START : START + WIDE[0], :]
    for index, step in enumerate(AROUND):
        strips[index].wait_recv()
        _, many_x, to_x = side(step[0], BX[0])
        _, many_y, to_y = side(step[1], BY[0])
        to_y += OY - 1 - START
        for half, target in enumerate((relaxed_low, relaxed_high)):
            low, high = max(to_x, 33 * half), min(to_x + many_x, 33 * half + 33)
            if low < high:
                target[low - 33 * half : high - 33 * half, to_y : to_y + many_y, :] += inbox[0, step][
                    low - to_x : high - to_x
                ]

    for step in range(1, N):
        slot = lax.rem(gx + N - step, N)
        line_copy("gx", step, slot).wait_recv()
    refs["gatherx"][gx] = refs["strip"][...]
    b4 = refs["b4"]
    b4[...] = jnp.zeros((80, 256), jnp.float32)
    for slot in range(N):
        for tile in range(2):
            at = (slice(6 + 4 * slot, 14 + 4 * slot), slice(LANES * tile, LANES * tile + LANES))
            b4[at] += refs["gatherx"][slot, 8 * tile : 8 * tile + 8, :]

    def times(one, other):
        return jnp.dot(
            one, other, precision=lax.Precision.HIGHEST, preferred_element_type=jnp.float32
        )

    sines_yz = refs["sines_yz"][...]
    waves = times(refs["sines_x"][8:72, :64], b4[8:72, :])
    waves = times(waves, sines_yz) * refs["gains"][...]
    waves = times(refs["sines_x"][pl.ds(6 + 4 * gx, 8), :64], waves)
    coarsest = times(waves, sines_yz)

    lane = lanes_of((8, LANES))
    back = lax.rem(16 - 16 * gy + 2 * LANES, LANES)
    place = lane + 16 * gy - 16
    near = pltpu.roll(coarsest[:, :LANES], back, 1)
    far = pltpu.roll(coarsest[:, LANES:], back, 1)
    mine = jnp.where((place >= 0) & (place < LANES), near, 0.0)
    mine = jnp.where((place >= LANES) & (place < 2 * LANES), far, mine)
    wide4 = times(mine, spreader[...])
    for place in range(6):
        refs["e4wide"][pl.ds(place, 8, stride=8), :] = wide4[:, place * LANES : (place + 1) * LANES]

    def correct(level, first, count, size):
        half = 6 if level == 3 else WIDE[level] // 2

        def body(coarse):
            if level == 3:
                fix = refs["e4wide"][...].reshape(8, 8, LANES)[:, :half]
            else:
                fix = e[level + 1][pl.ds(OX[level + 1] + coarse, size), OY - 2 : OY - 2 + half, :]
            fix = jnp.broadcast_to(fix[:, None], (size, 2, half, LANES)).reshape(2 * size, half, LANES)
            row = OX[level] + 2 * coarse
            for parity in range(2):
                place = (pl.ds(row, 2 * size), pl.ds(START + parity, half, stride=2), slice(None))
                x[level][place] = x[level][place] + fix
        chunks(first, count, size, body)

    correct(3, -2, 8, 8)
    relax(x[3], f[3], 3, WEIGHT_FIRST, 3, 14)
    relax(f[3], e[3], 3, WEIGHT_SECOND, 2, 12)
    correct(2, -2, 12, 6)
    relax(x[2], f[2], 2, WEIGHT_FIRST, 3, 11)
    relax(f[2], e[2], 2, WEIGHT_SECOND, 2, 10)
    correct(1, -2, 20, 4)
    relax(x[1], f[1], 1, WEIGHT_FIRST, 4, 4)
    relax(f[1], e[1], 1, WEIGHT_SECOND, 2, 4)

    for copy in sent:
        copy.wait_send()


def finish(
    e1, relaxed_low, relaxed_high, source_low, source_high, potential, residual, first, pot, out, out_sem
):
    relaxed = (relaxed_low, relaxed_high)
    source = (source_low, source_high)

    inside = inside_y(1, OY - 1, 18, FOUR_PI)

    def spread(coarse):
        rows = pl.ds(OX[1] + coarse, 17)
        cells = e1[rows, OY - 1 : OY + 17, :]
        same = (1.0 - WEIGHT_FIRST * 2.0 / 3.0) * cells + (WEIGHT_FIRST / 6.0) * along_z(cells, 0)
        same = same * inside
        share = inside * (WEIGHT_FIRST / 6.0)
        for odd_x in range(2):
            beside = e1[pl.ds(OX[1] + coarse + 2 * odd_x - 1, 17), OY - 1 : OY + 17, :]
            for odd_y in range(2):
                below = OY - 2 + 2 * odd_y
                both = beside + e1[rows, below : below + 18, :]
                both = same + share * both
                for index in range(17):
                    row = OX[0] + 2 * (coarse + index) + odd_x
                    first[row, pl.ds(OY - 2 + odd_y, 18, stride=2), :] = both[index]

    chunks(-1, 34, 17, spread)
    clip_x(first, 0, 2, START, WIDE[0])

    inside = inside_y(0, START, WIDE[0])
    cols = slice(START, START + WIDE[0])

    def second(row):
        center, total = around(first, row, 11, 0, START, WIDE[0])
        later = (1.0 - WEIGHT_SECOND) * center + (WEIGHT_SECOND / 6.0) * total
        place = row - OX[0] + 1
        pot[pl.ds(row, 11), cols, :] = (
            relaxed[place // 33][pl.ds(place % 33, 11)] + later
        ) * inside

    chunks(OX[0] - 1, BX[0] + 2, 11, second)
    clip_x(pot, 0, 1, START, WIDE[0])

    stores = []

    def store(origin, target, index, part):
        copy = pltpu.make_async_copy(
            origin, target.at[16 * part : 16 * part + 16], out_sem.at[index, part]
        )
        copy.start()
        stores.append(copy)

    for part in range(4):
        store(pot.at[4 + 16 * part : 20 + 16 * part, OY : OY + BY[0], :], potential, 0, part)

    def rest(row):
        center, total = around(pot, row, 8, 0, OY, BY[0])
        place = row - OX[0]
        out[pl.ds(place, 8)] = source[place // 32][pl.ds(place % 32, 8)] - 6.0 * center + total

    for part in range(4):
        chunks(4 + 16 * part, 16, 8, rest)
        store(out.at[16 * part : 16 * part + 16], residual, 1, part)
    for copy in stores:
        copy.wait()


def on_device(density):
    def cells(*shape):
        return pltpu.VMEM(shape + (LANES,), jnp.float32)

    level_arrays = [cells(ROWS[k], COLS[k]) for k in range(4)]
    dma = pltpu.SemaphoreType.DMA
    scratch = level_arrays * 6 + [
        cells(34, 40),
        cells(768),
        pltpu.VMEM((LANES, 768), jnp.float32),
        cells(64),
        cells(8),
        cells(N, 8),
        cells(16),
        cells(N, 16),
        pltpu.VMEM((80, 256), jnp.float32),
        cells(64),
        cells(80),
        pltpu.VMEM((256, 256), jnp.float32),
        pltpu.VMEM((64, 256), jnp.float32),
        cells(17, 32),
        cells(5, 24),
        cells(3, 24),
        dma((4,)),
        dma((8,)),
        dma((8,)),
        dma((30,)),
        dma((30,)),
        dma((N,)),
        dma((N,)),
        dma((N,)),
        dma((N,)),
    ]
    for dx, dy in AROUND:
        scratch.append(cells(SPREAD0 + 1 if dx else BX[0] + 2, SPREAD0 + 1 if dy else BY[0] + 2))
    for level in (1, 2, 3):
        for step in PARTNERS[level]:
            many_y = overlap(step[1], BY[level], SPREAD[level])[1]
            scratch.append(cells(groups(step[0], level)[1], many_y))
    hbm = pl.BlockSpec(memory_space=pltpu.HBM)
    vmem = pl.BlockSpec(memory_space=pltpu.VMEM)
    shapes = [(ROWS[1], COLS[1])] + [(33, WIDE[0])] * 2 + [(32, 32)] * 2
    shared = pl.pallas_call(
        kernel,
        out_shape=[jax.ShapeDtypeStruct(shape + (LANES,), jnp.float32) for shape in shapes],
        in_specs=[hbm],
        out_specs=[vmem] * 5,
        scratch_shapes=scratch,
        compiler_params=pltpu.CompilerParams(
            collective_id=0, has_side_effects=True, vmem_limit_bytes=50 * 2**20 + 2**18
        ),
        name="vcycle",
    )(density)
    return pl.pallas_call(
        finish,
        out_shape=[jax.ShapeDtypeStruct(density.shape, jnp.float32)] * 2,
        in_specs=[vmem] * 5,
        out_specs=[hbm] * 2,
        scratch_shapes=[
            cells(ROWS[0], COLS[0]),
            cells(ROWS[0], COLS[0]),
            cells(64, 32),
            dma((2, 4)),
        ],
        compiler_params=pltpu.CompilerParams(vmem_limit_bytes=24 * 2**20),
        name="finish",
    )(*shared)


def solution(mesh):
    return jax.shard_map(
        on_device,
        mesh=mesh,
        in_specs=(P("gx", "gy", None),),
        out_specs=(P("gx", "gy", None), P("gx", "gy", None)),
        check_vma=False,
    )
```
